128 devices in a mesh: blk: 16 (over x, y_lo, core), head: 8 (over y_hi, z).
Axes of the slice: x: 4, y: 4 (y_hi: 2, y_lo: 2; y = y_hi * 2 + y_lo), z: 4, core: 2. Of those that a mesh axis runs over, the one named last changes fastest.
Arguments:
- queries: bfloat16 [16384, 8192], P(('blk', 'head')), may hold values from -6 to 6
- keys: bfloat16 [16384, 1024], P(('blk', 'head')), may hold values from -6 to 6
- values: bfloat16 [16384, 1024], P(('blk', 'head')), may hold values from -6 to 6
- live_keys: int32 [16, 16, 16], replicated, may hold values from 0 to 63, as said below
- live_count: int32 [16, 16], replicated, may hold values from 1 to 16, as said below
Outputs:
- attended: bfloat16 [16384, 8192], P(('blk', 'head'))
The draws below stay inside these ranges and needn't reach their ends.
Inputs may be any that keep to these rules, and one draw needn't show every extreme that they name: live_keys[i, j, c] = a * 8 + b names the pair (query block i * 8 + a, key block j * 8 + b); the codes of one (i, j) are distinct, and a == b never occurs for i == j. Only slots c < live_count[i, j] are live. `live_count`: for every query shard i, some key shard j has all 16 slots live.
All inputs are finite; a program needn't handle non-finite values.
Results may differ from the reference program's by a relative error of at most 0.0065.
Values may be sent and summed in bfloat16 or wider, within the bound.
No kernel may reach another device: no remote copies, remote signals or barrier semaphores. Data moves between devices by JAX's collectives and lax.ppermute only.
A program may use at most 128 MiB of HBM per device.

```python
import jax
import jax.numpy as jnp
from jax import lax

HEADS = 64
KV_HEADS = 8
HEAD_DIM = 128
BLOCK = 128
SEQ = 16384
SHARD_BLOCKS = 8
PAIR_CAP = 16
N_BLK = 16


def base_field(key, width):
    return 1.5 * jax.random.truncated_normal(key, -4.0, 4.0, (SEQ, width), jnp.float32)


def draw_queries(key, part):
    field = base_field(jax.random.fold_in(key, 1), HEADS * HEAD_DIM)
    return field.astype(jnp.bfloat16)


def draw_keys(key, part):
    field = base_field(jax.random.fold_in(key, 2), KV_HEADS * HEAD_DIM)
    return field.astype(jnp.bfloat16)


def draw_live_keys(key, part):
    code_space = SHARD_BLOCKS * SHARD_BLOCKS
    raw_scores = jax.random.randint(jax.random.fold_in(key, 3), (N_BLK, N_BLK, code_space), 0, 2 ** 16)
    code_ids = jnp.arange(code_space, dtype=jnp.int32)
    ranking = raw_scores * code_space + code_ids[None, None, :]
    same_shard = jnp.arange(N_BLK)[:, None] == jnp.arange(N_BLK)[None, :]
    same_block = code_ids // SHARD_BLOCKS == code_ids % SHARD_BLOCKS
    ranking = ranking + jnp.where(same_shard[:, :, None] & same_block[None, None, :], 2 ** 30, 0)
    ordering = jnp.argsort(ranking, axis=-1)
    return ordering[:, :, :PAIR_CAP].astype(jnp.int32)


def draw_live_count(key, part):
    counts_drawn = jax.random.randint(jax.random.fold_in(key, 4), (N_BLK, N_BLK), 1, PAIR_CAP + 1)
    full_column = jax.random.randint(jax.random.fold_in(key, 5), (N_BLK,), 0, N_BLK)
    is_full = jnp.arange(N_BLK)[None, :] == full_column[:, None]
    return jnp.where(is_full, PAIR_CAP, counts_drawn).astype(jnp.int32)


def shard_levels(own_key, shape, split, smallest, largest):
    def one(axis_at, shards_of):
        heights = jax.random.uniform(jax.random.fold_in(jax.random.fold_in(own_key, 6), axis_at), (shards_of,), jnp.float32, smallest / len(split), largest / len(split))
        return jnp.repeat(jnp.exp(heights), shape[axis_at] // shards_of).reshape((-1,) + (1,) * (len(shape) - axis_at - 1))

    gain = one(*split[0])
    for cut in split[1:]:
        gain = gain * one(*cut)
    return gain


def bell_draw(key, extent, scale, most, split=(), kind=jnp.bfloat16):
    factor_of = shard_levels(key, extent, split, -0.22, 0.18) if split else 1.0
    result = jax.random.normal(key, extent, jnp.float32) * scale * factor_of
    return jnp.minimum(jnp.maximum(result, -most), most).astype(kind)


def setup_inputs(seed: int = 0) -> dict:
    splits = jax.random.split(jax.random.key(seed), 6)
    queries = draw_queries(jax.random.fold_in(splits[5], 71), 0)
    keys = draw_keys(jax.random.fold_in(splits[5], 71), 0)
    values = bell_draw(splits[2], (SEQ, KV_HEADS * HEAD_DIM), 1.0, 6.0, ((0, 128),))
    live_keys = draw_live_keys(jax.random.fold_in(splits[5], 71), 0)
    live_count = draw_live_count(jax.random.fold_in(splits[5], 71), 0)
    return dict(queries=queries, keys=keys, values=values, live_keys=live_keys, live_count=live_count)


def tile_scores(query_tiles, key_tiles):
    return jnp.einsum('ctkgd,cukd->ckgtu', query_tiles.astype(jnp.float32), key_tiles.astype(jnp.float32)) * (HEAD_DIM ** -0.5)


def rounded(weights):
    return lax.optimization_barrier(weights.astype(jnp.bfloat16)).astype(jnp.float32)


def reference(queries, keys, values, live_keys, live_count):
    group_count = HEADS // KV_HEADS
    shard_rows = SHARD_BLOCKS * BLOCK
    query_all = queries.reshape(N_BLK, SHARD_BLOCKS, BLOCK, KV_HEADS, group_count, HEAD_DIM)
    key_all = keys.reshape(N_BLK, SHARD_BLOCKS, BLOCK, KV_HEADS, HEAD_DIM)
    value_all = values.reshape(N_BLK, SHARD_BLOCKS, BLOCK, KV_HEADS, HEAD_DIM)
    slot_ids = jnp.arange(PAIR_CAP, dtype=jnp.int32)
    block_ids = jnp.arange(SHARD_BLOCKS, dtype=jnp.int32)
    shard_ids = jnp.arange(N_BLK, dtype=jnp.int32)

    def one_shard(shard_index):
        query_shard = query_all[shard_index]
        pair_codes = live_keys[shard_index]
        pair_counts = live_count[shard_index]
        diagonal = tile_scores(query_shard, key_all[shard_index])

        def build_tiles(kshard):
            slot_code = pair_codes[kshard]
            query_index = slot_code // SHARD_BLOCKS
            key_index = slot_code % SHARD_BLOCKS
            slot_valid = slot_ids < pair_counts[kshard]
            scores = tile_scores(query_shard[query_index], key_all[kshard][key_index])
            scores = jnp.where(slot_valid[:, None, None, None, None], scores, -jnp.inf)
            one_hot = (query_index[:, None] == block_ids[None, :]) & slot_valid[:, None]
            return scores, query_index, one_hot, key_index

        def max_step(row_max, kshard):
            scores, query_index, one_hot, key_index = build_tiles(kshard)
            tile_max = scores.max(-1)
            block_max = jnp.where(one_hot[:, :, None, None, None], tile_max[:, None], -jnp.inf).max(0)
            return jnp.maximum(row_max, block_max), None

        row_max, _ = lax.scan(max_step, diagonal.max(-1), shard_ids)
        diag_weights = jnp.exp(diagonal - row_max[..., None])
        denominator = diag_weights.sum(-1)
        weighted_sum = jnp.einsum('bkgtu,bukd->btkgd', rounded(diag_weights), value_all[shard_index].astype(jnp.float32))

        def sum_step(carried, kshard):
            denominator, weighted_sum = carried
            scores, query_index, one_hot, key_index = build_tiles(kshard)
            weights = jnp.exp(scores - row_max[query_index][..., None])
            hot_float = one_hot.astype(jnp.float32)
            denominator = denominator + jnp.einsum('cs,ckgt->skgt', hot_float, weights.sum(-1), precision=lax.Precision.HIGHEST)
            partial_sum = jnp.einsum('ckgtu,cukd->ctkgd', rounded(weights), value_all[kshard][key_index].astype(jnp.float32))
            weighted_sum = weighted_sum + jnp.einsum('cs,ctkgd->stkgd', hot_float, partial_sum, precision=lax.Precision.HIGHEST)
            return (denominator, weighted_sum), None

        (denominator, weighted_sum), _ = lax.scan(sum_step, (denominator, weighted_sum), shard_ids)
        normed = weighted_sum / denominator.transpose(0, 3, 1, 2)[..., None]
        return normed.astype(jnp.bfloat16).reshape(shard_rows, HEADS * HEAD_DIM)

    shards = lax.map(one_shard, shard_ids)
    return shards.reshape(SEQ, HEADS * HEAD_DIM)
```

```python
import functools

import jax
import jax.numpy as jnp
from jax import lax
from jax.experimental import pallas as pl
from jax.experimental.pallas import tpu as pltpu
from jax.sharding import PartitionSpec as P

HEADS = 64
KV_HEADS = 8
HEAD_DIM = 128
BLOCK = 128
LOG2E = 1.4426950408889634
CHUNK = 8
ROW_HEADS = 2


def plan_kernel(shard_ref, codes_ref, counts_ref, key_ref, value_ref, chunks_ref, fill_ref, *, blocks, shards, zero):
    shard = shard_ref[0]
    for a in range(blocks):
        own = shard * blocks + a
        key_ref[a, 0] = own
        value_ref[a, 0] = own
        fill_ref[a] = 1

    def visit_shard(j, _):
        def visit_slot(c, _):
            code = codes_ref[shard, j, c]
            a = lax.div(code, blocks)
            block = j * blocks + lax.rem(code, blocks)
            at = fill_ref[a]
            key_ref[a, at] = block
            value_ref[a, at] = block
            fill_ref[a] = at + 1
            return 0

        return lax.fori_loop(0, counts_ref[shard, j], visit_slot, 0)

    lax.fori_loop(0, shards, visit_shard, 0)
    for a in range(blocks):
        own = shard * blocks + a
        filled = fill_ref[a]
        chunks = lax.div(filled + CHUNK - 1, CHUNK)
        chunks_ref[a] = chunks

        def pad(at, _):
            key_ref[a, at] = own
            value_ref[a, at] = zero
            return 0

        lax.fori_loop(filled, chunks * CHUNK, pad, 0)


def plan(shard, live_keys, live_count, blocks, zero):
    shards = live_keys.shape[0]
    width = -(-(shards * blocks + 1) // CHUNK) * CHUNK
    smem = pl.BlockSpec(memory_space=pltpu.SMEM)
    return pl.pallas_call(
        functools.partial(plan_kernel, blocks=blocks, shards=shards, zero=zero),
        in_specs=[smem] * 3,
        out_specs=[smem] * 3,
        out_shape=[
            jax.ShapeDtypeStruct((blocks, width), jnp.int32),
            jax.ShapeDtypeStruct((blocks, width), jnp.int32),
            jax.ShapeDtypeStruct((blocks,), jnp.int32),
        ],
        scratch_shapes=[pltpu.SMEM((blocks,), jnp.int32)],
    )(shard[None].astype(jnp.int32), live_keys, live_count)


def attend_kernel(
    key_at, value_at, chunks, queries, keys_hbm, values_hbm, out, keys, values, total, peak, sem, *, heads
):
    b = pl.program_id(0)
    count = keys.shape[0]

    @pl.when(b == 0)
    def _():
        key_copy = pltpu.make_async_copy(keys_hbm, keys, sem.at[0])
        value_copy = pltpu.make_async_copy(
            values_hbm, values.at[pl.ds(0, count), :, pl.ds(0, HEAD_DIM)], sem.at[1]
        )
        key_copy.start()
        value_copy.start()
        values[pl.ds(0, count), :, pl.ds(HEAD_DIM, HEAD_DIM)] = jnp.ones(
            (count, BLOCK, HEAD_DIM), jnp.bfloat16
        )
        values[count] = jnp.zeros((BLOCK, 2 * HEAD_DIM), jnp.bfloat16)
        key_copy.wait()
        value_copy.wait()

    total[...] = jnp.zeros(total.shape, jnp.float32)
    peak[...] = jnp.full(peak.shape, -jnp.inf, jnp.float32)

    def visit(i, _):
        key_tile = jnp.concatenate([keys[key_at[b, i * CHUNK + c]] for c in range(CHUNK)], axis=0)
        value_tile = jnp.concatenate([values[value_at[b, i * CHUNK + c]] for c in range(CHUNK)], axis=0)
        for first in range(0, heads, ROW_HEADS):
            rows = slice(first * BLOCK, (first + ROW_HEADS) * BLOCK)
            query_tile = jnp.concatenate(
                [queries[:, h * HEAD_DIM : (h + 1) * HEAD_DIM] for h in range(first, first + ROW_HEADS)],
                axis=0,
            )
            scores = lax.dot_general(
                query_tile, key_tile, (((1,), (1,)), ((), ())), preferred_element_type=jnp.float32
            ) * (HEAD_DIM**-0.5 * LOG2E)
            old = peak[rows, :]
            new = jnp.maximum(old, jnp.max(scores, axis=1, keepdims=True))
            factor = jnp.exp2(old - new)
            weights = jnp.exp2(scores - jnp.concatenate([new] * CHUNK, axis=1)).astype(jnp.bfloat16)
            part = jnp.dot(weights, value_tile, preferred_element_type=jnp.float32)
            total[rows, :] = total[rows, :] * jnp.concatenate([factor, factor], axis=1) + part
            peak[rows, :] = new
        return 0

    lax.fori_loop(0, chunks[b], visit, 0)
    for h in range(heads):
        rows = total[h * BLOCK : (h + 1) * BLOCK, :]
        out[:, h * HEAD_DIM : (h + 1) * HEAD_DIM] = (rows[:, :HEAD_DIM] / rows[:, HEAD_DIM:]).astype(
            jnp.bfloat16
        )


def attend(queries, keys, values, lists):
    rows, width = queries.shape
    heads = width // HEAD_DIM
    count = keys.shape[0]
    return pl.pallas_call(
        functools.partial(attend_kernel, heads=heads),
        grid_spec=pltpu.PrefetchScalarGridSpec(
            num_scalar_prefetch=3,
            grid=(rows // BLOCK,),
            in_specs=[
                pl.BlockSpec((BLOCK, width), lambda b, *_: (b, 0)),
                pl.BlockSpec(memory_space=pl.ANY),
                pl.BlockSpec(memory_space=pl.ANY),
            ],
            out_specs=pl.BlockSpec((BLOCK, width), lambda b, *_: (b, 0)),
            scratch_shapes=[
                pltpu.VMEM((count, BLOCK, HEAD_DIM), jnp.bfloat16),
                pltpu.VMEM((count + 1, BLOCK, 2 * HEAD_DIM), jnp.bfloat16),
                pltpu.VMEM((heads * BLOCK, 2 * HEAD_DIM), jnp.float32),
                pltpu.VMEM((heads * BLOCK, HEAD_DIM), jnp.float32),
                pltpu.SemaphoreType.DMA((2,)),
            ],
        ),
        out_shape=jax.ShapeDtypeStruct((rows, width), jnp.bfloat16),
        compiler_params=pltpu.CompilerParams(vmem_limit_bytes=48 * 1024 * 1024),
    )(*lists, queries, keys, values)


def local(queries, keys, values, live_keys, live_count):
    parts = lax.axis_size("head")
    tokens = queries.shape[0]

    def spread(array):
        cut = array.reshape(tokens, parts, -1).transpose(1, 0, 2)
        moved = lax.all_to_all(cut, "head", split_axis=0, concat_axis=0, tiled=True)
        return moved.reshape(parts * tokens, -1)

    key_value = jnp.concatenate(
        [keys.reshape(tokens, parts, -1), values.reshape(tokens, parts, -1)], axis=2
    )
    key_value = spread(key_value)
    width = key_value.shape[1] // 2
    key_all = lax.all_gather(key_value[:, :width], "blk", axis=0, tiled=True)
    value_all = lax.all_gather(key_value[:, width:], "blk", axis=0, tiled=True)
    query_local = spread(queries)
    blocks = query_local.shape[0] // BLOCK
    count = key_all.shape[0] // BLOCK
    lists = plan(lax.axis_index("blk"), live_keys, live_count, blocks, count)
    attended = attend(
        query_local,
        key_all.reshape(count, BLOCK, -1),
        value_all.reshape(count, BLOCK, -1),
        lists,
    )
    back = lax.all_to_all(
        attended.reshape(parts, tokens, -1), "head", split_axis=0, concat_axis=0, tiled=True
    )
    return back.transpose(1, 0, 2).reshape(tokens, -1)


def solution(mesh):
    return jax.shard_map(
        local,
        mesh=mesh,
        in_specs=(
            P(("blk", "head"), None),
            P(("blk", "head"), None),
            P(("blk", "head"), None),
            P(),
            P(),
        ),
        out_specs=P(("blk", "head"), None),
        check_vma=False,
    )
```

```python
import functools

import jax
import jax.numpy as jnp
from jax import lax
from jax.experimental import pallas as pl
from jax.experimental.pallas import tpu as pltpu
from jax.sharding import PartitionSpec as P

HEADS = 64
KV_HEADS = 8
HEAD_DIM = 128
BLOCK = 128
LOG2E = 1.4426950408889634
CHUNK = 8
ROW_HEADS = 2
HEAD_PARTS = 2


def plan_kernel(shard_ref, codes_ref, counts_ref, key_ref, value_ref, chunks_ref, fill_ref, *, blocks, shards, zero):
    shard = shard_ref[0]
    for a in range(blocks):
        fill_ref[a] = 0

    def append(a, block):
        at = fill_ref[a]
        key_ref[a, at] = block
        value_ref[a, at] = block
        fill_ref[a] = at + 1

    def visit_shard(j, _):
        @pl.when(j == shard)
        def _():
            for a in range(blocks):
                append(a, shard * blocks + a)

        def visit_slot(c, _):
            code = codes_ref[shard, j, c]
            append(lax.div(code, blocks), j * blocks + lax.rem(code, blocks))
            return 0

        return lax.fori_loop(0, counts_ref[shard, j], visit_slot, 0)

    lax.fori_loop(0, shards, visit_shard, 0)
    for a in range(blocks):
        own = shard * blocks + a
        filled = fill_ref[a]
        chunks = lax.div(filled + CHUNK - 1, CHUNK)
        chunks_ref[a] = chunks

        def pad(at, _):
            key_ref[a, at] = own
            value_ref[a, at] = zero
            return 0

        lax.fori_loop(filled, chunks * CHUNK, pad, 0)


def plan(shard, live_keys, live_count, blocks, zero):
    shards = live_keys.shape[0]
    width = -(-(shards * blocks + 1) // CHUNK) * CHUNK
    smem = pl.BlockSpec(memory_space=pltpu.SMEM)
    return pl.pallas_call(
        functools.partial(plan_kernel, blocks=blocks, shards=shards, zero=zero),
        in_specs=[smem] * 3,
        out_specs=[smem] * 3,
        out_shape=[
            jax.ShapeDtypeStruct((blocks, width), jnp.int32),
            jax.ShapeDtypeStruct((blocks, width), jnp.int32),
            jax.ShapeDtypeStruct((blocks,), jnp.int32),
        ],
        scratch_shapes=[pltpu.SMEM((blocks,), jnp.int32)],
        cost_estimate=pl.CostEstimate(flops=0, bytes_accessed=20_000_000, transcendentals=0),
    )(shard[None].astype(jnp.int32), live_keys, live_count)


def attend_kernel(
    key_at, value_at, chunks, queries, gathered, out, pairs, ones, total, peak, ready, sem, *, heads, shards
):
    b = pl.program_id(0)
    count = pairs.shape[0] - 1
    span = count // shards

    def arrival(j):
        part = pl.ds(j * span, span)
        return pltpu.make_async_copy(gathered.at[part], pairs.at[part], sem.at[j])

    @pl.when(b == 0)
    def _():
        def begin(j, _):
            arrival(j).start()
            return 0

        lax.fori_loop(0, shards, begin, 0)
        ready[0] = 0
        ones[0] = jnp.ones(ones.shape[1:], jnp.bfloat16)
        ones[1] = jnp.zeros(ones.shape[1:], jnp.bfloat16)
        pairs[count] = jnp.zeros(pairs.shape[1:], jnp.bfloat16)

    total[...] = jnp.zeros(total.shape, jnp.float32)
    peak[...] = jnp.full(peak.shape, -jnp.inf, jnp.float32)

    def visit(i, _):
        @pl.when(b == 0)
        def _():
            last = lax.div(key_at[b, i * CHUNK + CHUNK - 1], span) + 1
            needed = jnp.where(i == chunks[b] - 1, shards, last)

            def finish(j, _):
                arrival(j).wait()
                return 0

            lax.fori_loop(ready[0], needed, finish, 0)
            ready[0] = jnp.maximum(ready[0], needed)

        key_tile = jnp.concatenate(
            [pairs[key_at[b, i * CHUNK + c], :, :HEAD_DIM] for c in range(CHUNK)], axis=0
        )
        slots = [value_at[b, i * CHUNK + c] for c in range(CHUNK)]
        value_tile = jnp.concatenate(
            [
                jnp.concatenate([pairs[s, :, HEAD_DIM:] for s in slots], axis=0),
                jnp.concatenate([ones[(s == count).astype(jnp.int32)] for s in slots], axis=0),
            ],
            axis=1,
        )
        for first in range(0, heads, ROW_HEADS):
            rows = slice(first * BLOCK, (first + ROW_HEADS) * BLOCK)
            query_tile = jnp.concatenate(
                [queries[:, h * HEAD_DIM : (h + 1) * HEAD_DIM] for h in range(first, first + ROW_HEADS)],
                axis=0,
            )
            scores = lax.dot_general(
                query_tile, key_tile, (((1,), (1,)), ((), ())), preferred_element_type=jnp.float32
            ) * (HEAD_DIM**-0.5 * LOG2E)
            old = peak[rows, :]
            new = jnp.maximum(old, jnp.max(scores, axis=1, keepdims=True))
            factor = jnp.exp2(old - new)
            weights = jnp.exp2(scores - jnp.concatenate([new] * CHUNK, axis=1)).astype(jnp.bfloat16)
            part = jnp.dot(weights, value_tile, preferred_element_type=jnp.float32)
            total[rows, :] = total[rows, :] * jnp.concatenate([factor, factor], axis=1) + part
            peak[rows, :] = new
        return 0

    lax.fori_loop(0, chunks[b], visit, 0)
    for h in range(heads):
        rows = total[h * BLOCK : (h + 1) * BLOCK, :]
        out[:, h * HEAD_DIM : (h + 1) * HEAD_DIM] = (rows[:, :HEAD_DIM] / rows[:, HEAD_DIM:]).astype(
            jnp.bfloat16
        )


def attend(queries, gathered, lists, shards, part, parts):
    rows, all_width = queries.shape
    width = all_width // parts
    heads = width // HEAD_DIM
    count = gathered.shape[0]
    pair_estimate = 180 * 2 * 2 * heads * BLOCK * BLOCK * HEAD_DIM
    return pl.pallas_call(
        functools.partial(attend_kernel, heads=heads, shards=shards),
        grid_spec=pltpu.PrefetchScalarGridSpec(
            num_scalar_prefetch=3,
            grid=(rows // BLOCK,),
            in_specs=[
                pl.BlockSpec((BLOCK, width), lambda b, *_: (b, part)),
                pl.BlockSpec(memory_space=pl.ANY),
            ],
            out_specs=pl.BlockSpec((BLOCK, width), lambda b, *_: (b, 0)),
            scratch_shapes=[
                pltpu.VMEM((count + 1, BLOCK, 2 * HEAD_DIM), jnp.bfloat16),
                pltpu.VMEM((2, BLOCK, HEAD_DIM), jnp.bfloat16),
                pltpu.VMEM((heads * BLOCK, 2 * HEAD_DIM), jnp.float32),
                pltpu.VMEM((heads * BLOCK, HEAD_DIM), jnp.float32),
                pltpu.SMEM((1,), jnp.int32),
                pltpu.SemaphoreType.DMA((shards,)),
            ],
        ),
        out_shape=jax.ShapeDtypeStruct((rows, width), jnp.bfloat16),
        compiler_params=pltpu.CompilerParams(vmem_limit_bytes=48 * 1024 * 1024),
        cost_estimate=pl.CostEstimate(flops=pair_estimate * 3, bytes_accessed=12_000_000, transcendentals=0),
    )(*lists, queries, gathered)


def local(queries, keys, values, live_keys, live_count):
    parts = lax.axis_size("head")
    tokens = queries.shape[0]

    def spread(array):
        cut = array.reshape(tokens, parts, -1).transpose(1, 0, 2)
        moved = lax.all_to_all(cut, "head", split_axis=0, concat_axis=0, tiled=True)
        return moved.reshape(parts * tokens, -1)

    key_value = spread(
        jnp.concatenate([keys.reshape(tokens, parts, -1), values.reshape(tokens, parts, -1)], axis=2)
    )
    gathered = lax.all_gather(key_value, "blk", axis=0, tiled=True)
    query_local = spread(queries)
    blocks = query_local.shape[0] // BLOCK
    count = gathered.shape[0] // BLOCK
    lists = plan(lax.axis_index("blk"), live_keys, live_count, blocks, count)
    gathered = gathered.reshape(count, BLOCK, -1)
    backs = []
    for part in range(HEAD_PARTS):
        attended = attend(query_local, gathered, lists, live_keys.shape[0], part, HEAD_PARTS)
        backs.append(
            lax.all_to_all(
                attended.reshape(parts, tokens, -1), "head", split_axis=0, concat_axis=0, tiled=True
            )
        )
    back = jnp.concatenate(backs, axis=2)
    return back.transpose(1, 0, 2).reshape(tokens, -1)


def solution(mesh):
    return jax.shard_map(
        local,
        mesh=mesh,
        in_specs=(
            P(("blk", "head"), None),
            P(("blk", "head"), None),
            P(("blk", "head"), None),
            P(),
            P(),
        ),
        out_specs=P(("blk", "head"), None),
        check_vma=False,
    )
```

```python
import functools

import jax
import jax.numpy as jnp
from jax import lax
from jax.experimental import pallas as pl
from jax.experimental.pallas import tpu as pltpu
from jax.sharding import Mesh
from jax.sharding import PartitionSpec as P

HEADS = 64
KV_HEADS = 8
HEAD_DIM = 128
BLOCK = 128
LOG2E = 1.4426950408889634
CHUNK = 8
ROW_HEADS = 2
HEAD_PARTS = 2


def plan_kernel(place_ref, codes_ref, counts_ref, key_ref, value_ref, chunks_ref, fill_ref, *, blocks, sizes, zero):
    x_size, y_size, core_size = sizes
    x, y, core = place_ref[0], place_ref[1], place_ref[2]
    shard = (x * y_size + y) * core_size + core
    for a in range(blocks):
        key_ref[a, 0] = a
        value_ref[a, 0] = a
        fill_ref[a] = 1

    def visit_shard(slot, _):
        from_x = lax.rem(x + lax.rem(slot, x_size), x_size)
        from_y = lax.rem(y + lax.rem(lax.div(slot, x_size), y_size), y_size)
        from_core = lax.rem(core + lax.div(slot, x_size * y_size), core_size)
        j = (from_x * y_size + from_y) * core_size + from_core

        def visit_entry(c, _):
            code = codes_ref[shard, j, c]
            a = lax.div(code, blocks)
            block = slot * blocks + lax.rem(code, blocks)
            at = fill_ref[a]
            key_ref[a, at] = block
            value_ref[a, at] = block
            fill_ref[a] = at + 1
            return 0

        return lax.fori_loop(0, counts_ref[shard, j], visit_entry, 0)

    lax.fori_loop(0, x_size * y_size * core_size, visit_shard, 0)
    for a in range(blocks):
        filled = fill_ref[a]
        chunks = lax.div(filled + CHUNK - 1, CHUNK)
        chunks_ref[a] = chunks

        def pad(at, _):
            key_ref[a, at] = a
            value_ref[a, at] = zero
            return 0

        lax.fori_loop(filled, chunks * CHUNK, pad, 0)


def plan(place, live_keys, live_count, blocks, sizes, zero):
    shards = live_keys.shape[0]
    width = -(-(shards * blocks + 1) // CHUNK) * CHUNK
    smem = pl.BlockSpec(memory_space=pltpu.SMEM)
    return pl.pallas_call(
        functools.partial(plan_kernel, blocks=blocks, sizes=sizes, zero=zero),
        in_specs=[smem] * 3,
        out_specs=[smem] * 3,
        out_shape=[
            jax.ShapeDtypeStruct((blocks, width), jnp.int32),
            jax.ShapeDtypeStruct((blocks, width), jnp.int32),
            jax.ShapeDtypeStruct((blocks,), jnp.int32),
        ],
        scratch_shapes=[pltpu.SMEM((blocks,), jnp.int32)],
        cost_estimate=pl.CostEstimate(flops=0, bytes_accessed=20_000_000, transcendentals=0),
    )(place, live_keys, live_count)


def attend_kernel(
    key_at, value_at, chunks, queries, *refs, heads, shards
):
    pieces, (out, pairs, ones, total, peak, ready, sem) = refs[:shards], refs[shards:]
    b = pl.program_id(0)
    count = pairs.shape[0] - 1
    span = count // shards

    def arrival(j):
        part = pl.ds(j * span, span)
        return pltpu.make_async_copy(pieces[j], pairs.at[part], sem.at[j])

    @pl.when(b == 0)
    def _():
        for j in range(shards):
            arrival(j).start()
        ready[0] = 0
        ones[0] = jnp.ones(ones.shape[1:], jnp.bfloat16)
        ones[1] = jnp.zeros(ones.shape[1:], jnp.bfloat16)
        pairs[count] = jnp.zeros(pairs.shape[1:], jnp.bfloat16)

    total[...] = jnp.zeros(total.shape, jnp.float32)
    peak[...] = jnp.full(peak.shape, -jnp.inf, jnp.float32)

    def visit(i, _):
        @pl.when(b == 0)
        def _():
            last = lax.div(key_at[b, i * CHUNK + CHUNK - 1], span) + 1
            needed = jnp.where(i == chunks[b] - 1, shards, last)

            for j in range(shards):

                @pl.when((j >= ready[0]) & (j < needed))
                def _():
                    arrival(j).wait()

            ready[0] = jnp.maximum(ready[0], needed)

        key_tile = jnp.concatenate(
            [pairs[key_at[b, i * CHUNK + c], :, :HEAD_DIM] for c in range(CHUNK)], axis=0
        )
        slots = [value_at[b, i * CHUNK + c] for c in range(CHUNK)]
        value_tile = jnp.concatenate(
            [
                jnp.concatenate([pairs[s, :, HEAD_DIM:] for s in slots], axis=0),
                jnp.concatenate([ones[(s == count).astype(jnp.int32)] for s in slots], axis=0),
            ],
            axis=1,
        )
        for first in range(0, heads, ROW_HEADS):
            rows = slice(first * BLOCK, (first + ROW_HEADS) * BLOCK)
            query_tile = jnp.concatenate(
                [queries[:, h * HEAD_DIM : (h + 1) * HEAD_DIM] for h in range(first, first + ROW_HEADS)],
                axis=0,
            )
            scores = lax.dot_general(
                query_tile, key_tile, (((1,), (1,)), ((), ())), preferred_element_type=jnp.float32
            ) * (HEAD_DIM**-0.5 * LOG2E)
            old = peak[rows, :]
            new = jnp.maximum(old, jnp.max(scores, axis=1, keepdims=True))
            factor = jnp.exp2(old - new)
            weights = jnp.exp2(scores - jnp.concatenate([new] * CHUNK, axis=1)).astype(jnp.bfloat16)
            part = jnp.dot(weights, value_tile, preferred_element_type=jnp.float32)
            total[rows, :] = total[rows, :] * jnp.concatenate([factor, factor], axis=1) + part
            peak[rows, :] = new
        return 0

    lax.fori_loop(0, chunks[b], visit, 0)
    for h in range(heads):
        rows = total[h * BLOCK : (h + 1) * BLOCK, :]
        out[:, h * HEAD_DIM : (h + 1) * HEAD_DIM] = (rows[:, :HEAD_DIM] / rows[:, HEAD_DIM:]).astype(
            jnp.bfloat16
        )


def attend(queries, pieces, lists, part, parts):
    rows, all_width = queries.shape
    width = all_width // parts
    heads = width // HEAD_DIM
    shards = len(pieces)
    span = pieces[0].shape[0] // BLOCK
    count = shards * span
    pieces = [piece.reshape(span, BLOCK, -1) for piece in pieces]
    pair_estimate = 180 * 2 * 2 * heads * BLOCK * BLOCK * HEAD_DIM
    return pl.pallas_call(
        functools.partial(attend_kernel, heads=heads, shards=shards),
        grid_spec=pltpu.PrefetchScalarGridSpec(
            num_scalar_prefetch=3,
            grid=(rows // BLOCK,),
            in_specs=[pl.BlockSpec((BLOCK, width), lambda b, *_: (b, part))]
            + [pl.BlockSpec(memory_space=pl.ANY)] * shards,
            out_specs=pl.BlockSpec((BLOCK, width), lambda b, *_: (b, 0)),
            scratch_shapes=[
                pltpu.VMEM((count + 1, BLOCK, 2 * HEAD_DIM), jnp.bfloat16),
                pltpu.VMEM((2, BLOCK, HEAD_DIM), jnp.bfloat16),
                pltpu.VMEM((heads * BLOCK, 2 * HEAD_DIM), jnp.float32),
                pltpu.VMEM((heads * BLOCK, HEAD_DIM), jnp.float32),
                pltpu.SMEM((1,), jnp.int32),
                pltpu.SemaphoreType.DMA((shards,)),
            ],
        ),
        out_shape=jax.ShapeDtypeStruct((rows, width), jnp.bfloat16),
        compiler_params=pltpu.CompilerParams(vmem_limit_bytes=48 * 1024 * 1024),
        cost_estimate=pl.CostEstimate(flops=pair_estimate * 3, bytes_accessed=12_000_000, transcendentals=0),
    )(*lists, queries, *pieces)


def gather_shards(own):
    def shift(array, axis, step):
        size = lax.axis_size(axis)
        return lax.ppermute(array, axis, [(i, (i + step) % size) for i in range(size)])

    here = [own, shift(own, "x", -1), None, shift(own, "x", 1)]
    across = shift(own, "y_lo", 1)
    here[2] = shift(here[3], "x", 1)
    there = [across, shift(across, "x", -1), None, shift(across, "x", 1)]
    there[2] = shift(there[1], "x", -1)
    near = here + there
    return near + [shift(piece, "core", 1) for piece in near]


def local(queries, keys, values, live_keys, live_count):
    head_axes = ("y_hi", "z")
    parts = lax.axis_size(head_axes)
    tokens = queries.shape[0]

    def spread(array):
        cut = array.reshape(tokens, parts, -1).transpose(1, 0, 2)
        moved = lax.all_to_all(cut, head_axes, split_axis=0, concat_axis=0, tiled=True)
        return moved.reshape(parts * tokens, -1)

    key_value = spread(
        jnp.concatenate([keys.reshape(tokens, parts, -1), values.reshape(tokens, parts, -1)], axis=2)
    )
    pieces = gather_shards(key_value)
    query_local = spread(queries)
    blocks = query_local.shape[0] // BLOCK
    blk_axes = ("x", "y_lo", "core")
    place = jnp.stack([lax.axis_index(axis) for axis in blk_axes]).astype(jnp.int32)
    sizes = tuple(lax.axis_size(axis) for axis in blk_axes)
    lists = plan(place, live_keys, live_count, blocks, sizes, len(pieces) * blocks)
    backs = []
    for part in range(HEAD_PARTS):
        attended = attend(query_local, pieces, lists, part, HEAD_PARTS)
        backs.append(
            lax.all_to_all(
                attended.reshape(parts, tokens, -1), head_axes, split_axis=0, concat_axis=0, tiled=True
            )
        )
    back = jnp.concatenate(backs, axis=2)
    return back.transpose(1, 0, 2).reshape(tokens, -1)


def solution(mesh):
    fine = Mesh(mesh.devices.reshape(4, 2, 2, 2, 4), ("x", "y_lo", "core", "y_hi", "z"))
    rows = P(("x", "y_lo", "core", "y_hi", "z"), None)
    return jax.shard_map(
        local,
        mesh=fine,
        in_specs=(rows, rows, rows, P(), P()),
        out_specs=rows,
        check_vma=False,
    )
```

```python
import functools

import jax
import jax.numpy as jnp
from jax import lax
from jax.experimental import pallas as pl
from jax.experimental.pallas import tpu as pltpu
from jax.sharding import Mesh
from jax.sharding import PartitionSpec as P

HEADS = 64
KV_HEADS = 8
HEAD_DIM = 128
BLOCK = 128
LOG2E = 1.4426950408889634
CHUNK = 4
GROUP_HEADS = 2
PIECE = 512


def plan_kernel(place_ref, codes_ref, counts_ref, key_ref, value_ref, chunks_ref, fill_ref, *, blocks, sizes, zero):
    x_size, y_size, core_size = sizes
    x, y, core = place_ref[0], place_ref[1], place_ref[2]
    shard = (x * y_size + y) * core_size + core
    for a in range(blocks):
        key_ref[a, 0] = a
        value_ref[a, 0] = a
        fill_ref[a] = 1

    def visit_shard(slot, _):
        from_x = lax.rem(x + lax.rem(slot, x_size), x_size)
        from_y = lax.rem(y + lax.rem(lax.div(slot, x_size), y_size), y_size)
        from_core = lax.rem(core + lax.div(slot, x_size * y_size), core_size)
        j = (from_x * y_size + from_y) * core_size + from_core

        def visit_entry(c, _):
            code = codes_ref[shard, j, c]
            a = lax.div(code, blocks)
            block = slot * blocks + lax.rem(code, blocks)
            at = fill_ref[a]
            key_ref[a, at] = block
            value_ref[a, at] = block
            fill_ref[a] = at + 1
            return 0

        return lax.fori_loop(0, counts_ref[shard, j], visit_entry, 0)

    lax.fori_loop(0, x_size * y_size * core_size, visit_shard, 0)
    for a in range(blocks):
        filled = fill_ref[a]
        chunks = lax.div(filled + CHUNK - 1, CHUNK)
        chunks_ref[a] = chunks

        def pad(at, _):
            key_ref[a, at] = a
            value_ref[a, at] = zero
            return 0

        lax.fori_loop(filled, chunks * CHUNK, pad, 0)


def plan(place, live_keys, live_count, blocks, sizes, zero):
    shards = live_keys.shape[0]
    width = -(-(shards * blocks + 1) // CHUNK) * CHUNK
    smem = pl.BlockSpec(memory_space=pltpu.SMEM)
    return pl.pallas_call(
        functools.partial(plan_kernel, blocks=blocks, sizes=sizes, zero=zero),
        in_specs=[smem] * 3,
        out_specs=[smem] * 3,
        out_shape=[
            jax.ShapeDtypeStruct((blocks, width), jnp.int32),
            jax.ShapeDtypeStruct((blocks, width), jnp.int32),
            jax.ShapeDtypeStruct((blocks,), jnp.int32),
        ],
        scratch_shapes=[pltpu.SMEM((blocks,), jnp.int32)],
        cost_estimate=pl.CostEstimate(flops=0, bytes_accessed=20_000_000, transcendentals=0),
    )(place, live_keys, live_count)


def attend_kernel(key_at, value_at, chunks, queries, *refs, heads, shards):
    pieces, (out, pairs, ones, total, peak, scaled, *rest) = refs[:shards], refs[shards:]
    groups = heads // GROUP_HEADS
    raw, soft, (level, fade, late_fade, ready, sem) = rest[:groups], rest[groups : groups + 2], rest[groups + 2 :]
    b = pl.program_id(0)
    count = pairs.shape[0] - 1
    span = count // shards
    width = GROUP_HEADS * BLOCK
    scale = HEAD_DIM**-0.5 * LOG2E

    def arrival(j):
        return pltpu.make_async_copy(pieces[j], pairs.at[pl.ds(j * span, span)], sem.at[j])

    @pl.when(b == 0)
    def _():
        for j in range(shards):
            arrival(j).start()
        ready[0] = 0
        ones[0] = jnp.ones(ones.shape[1:], jnp.bfloat16)
        ones[1] = jnp.zeros(ones.shape[1:], jnp.bfloat16)
        pairs[count] = jnp.zeros(pairs.shape[1:], jnp.bfloat16)

    def arrive(i):
        @pl.when(b == 0)
        def _():
            last = lax.div(key_at[b, i * CHUNK + CHUNK - 1], span) + 1
            needed = jnp.where(i >= chunks[b] - 1, shards, last)
            for j in range(shards):

                @pl.when((j >= ready[0]) & (j < needed))
                def _():
                    arrival(j).wait()

            ready[0] = jnp.maximum(ready[0], needed)

    def keys_of(i):
        return jnp.concatenate(
            [pairs[key_at[b, i * CHUNK + c], :, :HEAD_DIM] for c in range(CHUNK)], axis=0
        )

    def values_of(i):
        slots = [value_at[b, i * CHUNK + c] for c in range(CHUNK)]
        return jnp.concatenate(
            [
                jnp.concatenate([pairs[s, :, HEAD_DIM:] for s in slots], axis=1),
                jnp.concatenate([ones[(s == count).astype(jnp.int32)] for s in slots], axis=1),
            ],
            axis=0,
        )

    cuts = [slice(j * PIECE, (j + 1) * PIECE) for j in range(CHUNK * BLOCK // PIECE)]

    def columns(g):
        return slice(g * width, (g + 1) * width)

    def score(keys, g):
        return lax.dot_general(
            jnp.concatenate([keys, keys], axis=1),
            scaled[columns(g), :],
            (((1,), (1,)), ((), ())),
            preferred_element_type=jnp.float32,
        )

    def partial_max(piece):
        return jnp.max(piece.reshape(-1, 8, width), axis=0)

    for h in range(heads):
        at = slice(h * BLOCK, (h + 1) * BLOCK)
        exact = queries[:, h * HEAD_DIM : (h + 1) * HEAD_DIM].astype(jnp.float32) * scale
        high = exact.astype(jnp.bfloat16)
        scaled[at, :HEAD_DIM] = high
        scaled[at, HEAD_DIM:] = (exact - high.astype(jnp.float32)).astype(jnp.bfloat16)
    total[...] = jnp.zeros(total.shape, jnp.float32)
    peak[...] = jnp.full(peak.shape, -jnp.inf, jnp.float32)
    soft[1][...] = jnp.zeros(soft[1].shape, jnp.bfloat16)
    late_fade[...] = jnp.ones(late_fade.shape, jnp.float32)
    arrive(0)
    keys = keys_of(0)
    for g in range(2):
        raw[g][...] = score(keys, g)
    level[...] = jnp.max(partial_max(raw[0][...]), axis=0, keepdims=True)
    peak[:, columns(0)] = level[...]
    fade[...] = jnp.zeros(fade.shape, jnp.float32)
    end = chunks[b]

    def visit(i, _):
        following = jnp.minimum(i + 1, end - 1)
        arrive(following)
        keys = keys_of(i)
        next_keys = keys_of(following)
        values = values_of(i)
        before = values_of(jnp.maximum(i - 1, 0))
        new, factor, late = level[...], fade[...], late_fade[...]
        for g in range(groups):
            ahead, upcoming, done = (g + 2) % groups, (g + 1) % groups, (g - 1) % groups
            source = keys if g + 2 < groups else next_keys
            multiplier = values if g else before
            into = columns(done)
            total[:, into] = total[:, into] * late
            tops = None
            for cut in cuts:
                raw[ahead][cut, :] = score(source[cut, :], ahead)
                soft[g % 2][cut, :] = jnp.exp2(raw[g][cut, :] - new).astype(jnp.bfloat16)
                total[:, into] += jnp.dot(
                    multiplier[:, cut], soft[(g + 1) % 2][cut, :], preferred_element_type=jnp.float32
                )
                most = partial_max(raw[upcoming][cut, :])
                tops = most if tops is None else jnp.maximum(tops, most)
            at = columns(upcoming)
            old = peak[:, at]
            new = jnp.maximum(old, jnp.max(tops, axis=0, keepdims=True))
            peak[:, at] = new
            factor, late = jnp.exp2(old - new), factor
        level[...] = new
        fade[...] = factor
        late_fade[...] = late
        return 0

    lax.fori_loop(0, end, visit, 0)
    at = columns(groups - 1)
    total[:, at] = total[:, at] * late_fade[...] + jnp.dot(
        values_of(end - 1), soft[1][...], preferred_element_type=jnp.float32
    )
    square = (BLOCK, BLOCK)
    unit = (
        lax.broadcasted_iota(jnp.int32, square, 0) == lax.broadcasted_iota(jnp.int32, square, 1)
    ).astype(jnp.bfloat16)
    for h in range(heads):
        at = slice(h * BLOCK, (h + 1) * BLOCK)
        normed = (total[:HEAD_DIM, at] / total[HEAD_DIM : HEAD_DIM + 1, at]).astype(jnp.bfloat16)
        turned = lax.dot_general(
            unit, normed, (((1,), (1,)), ((), ())), preferred_element_type=jnp.float32
        )
        out[:, h * HEAD_DIM : (h + 1) * HEAD_DIM] = turned.astype(jnp.bfloat16)


def attend(queries, pieces, lists):
    rows, width = queries.shape
    heads = width // HEAD_DIM
    shards = len(pieces)
    span = pieces[0].shape[0] // BLOCK
    count = shards * span
    pieces = [piece.reshape(span, BLOCK, -1) for piece in pieces]
    pair_estimate = 180 * 2 * 2 * heads * BLOCK * BLOCK * HEAD_DIM
    return pl.pallas_call(
        functools.partial(attend_kernel, heads=heads, shards=shards),
        grid_spec=pltpu.PrefetchScalarGridSpec(
            num_scalar_prefetch=3,
            grid=(rows // BLOCK,),
            in_specs=[pl.BlockSpec((BLOCK, width), lambda b, *_: (b, 0))]
            + [pl.BlockSpec(memory_space=pl.ANY)] * shards,
            out_specs=pl.BlockSpec((BLOCK, width), lambda b, *_: (b, 0)),
            scratch_shapes=[
                pltpu.VMEM((count + 1, BLOCK, 2 * HEAD_DIM), jnp.bfloat16),
                pltpu.VMEM((2, 16, BLOCK), jnp.bfloat16),
                pltpu.VMEM((HEAD_DIM + 16, heads * BLOCK), jnp.float32),
                pltpu.VMEM((1, heads * BLOCK), jnp.float32),
                pltpu.VMEM((heads * BLOCK, 2 * HEAD_DIM), jnp.bfloat16),
            ]
            + [pltpu.VMEM((CHUNK * BLOCK, GROUP_HEADS * BLOCK), jnp.float32)] * (heads // GROUP_HEADS)
            + [pltpu.VMEM((CHUNK * BLOCK, GROUP_HEADS * BLOCK), jnp.bfloat16)] * 2
            + [pltpu.VMEM((1, GROUP_HEADS * BLOCK), jnp.float32)] * 3
            + [
                pltpu.SMEM((1,), jnp.int32),
                pltpu.SemaphoreType.DMA((shards,)),
            ],
        ),
        out_shape=jax.ShapeDtypeStruct((rows, width), jnp.bfloat16),
        compiler_params=pltpu.CompilerParams(vmem_limit_bytes=48 * 1024 * 1024),
        cost_estimate=pl.CostEstimate(flops=pair_estimate * 3, bytes_accessed=12_000_000, transcendentals=0),
    )(*lists, queries, *pieces)


def shift(array, axis, step):
    size = lax.axis_size(axis)
    return lax.ppermute(array, axis, [(i, (i + step) % size) for i in range(size)])


def gather_shards(own, meanwhile):
    here = [own, shift(own, "x", -1), None, shift(own, "x", 1)]
    across = shift(own, "y_lo", 1)
    here[3], across, result = lax.optimization_barrier((here[3], across, meanwhile()))
    here[2] = shift(here[3], "x", 1)
    there = [across, shift(across, "x", -1), None, shift(across, "x", 1)]
    there[2] = shift(there[1], "x", -1)
    near = here + there
    return near + [shift(piece, "core", 1) for piece in near], result


def local(queries, keys, values, live_keys, live_count):
    head_axes, blk_axes = ("y_hi", "z"), ("x", "y_lo", "core")
    parts = lax.axis_size(head_axes)
    tokens = queries.shape[0]
    sizes = tuple(lax.axis_size(axis) for axis in blk_axes)
    blocks = parts * tokens // BLOCK

    def exchange(cut):
        moved = lax.all_to_all(cut, head_axes, split_axis=0, concat_axis=0, tiled=True)
        return moved.reshape(parts * tokens, -1)

    def cut(array):
        return array.reshape(tokens, parts, -1)

    own = exchange(
        jnp.concatenate([cut(keys).transpose(1, 0, 2), cut(values).transpose(1, 2, 0)], axis=2)
    )
    place = jnp.stack([lax.axis_index(axis) for axis in blk_axes]).astype(jnp.int32)
    own, place = lax.optimization_barrier((own, place))
    zero = live_keys.shape[0] * blocks
    pieces, lists = gather_shards(own, lambda: plan(place, live_keys, live_count, blocks, sizes, zero))
    query_local = exchange(cut(queries).transpose(1, 0, 2))
    attended = attend(query_local, pieces, lists)
    back = lax.all_to_all(
        attended.reshape(parts, tokens, -1), head_axes, split_axis=0, concat_axis=0, tiled=True
    )
    return back.transpose(1, 0, 2).reshape(tokens, -1)


def solution(mesh):
    fine = Mesh(mesh.devices.reshape(4, 2, 2, 2, 4), ("x", "y_lo", "core", "y_hi", "z"))
    rows = P(("x", "y_lo", "core", "y_hi", "z"), None)
    return jax.shard_map(
        local,
        mesh=fine,
        in_specs=(rows, rows, rows, P(), P()),
        out_specs=rows,
        check_vma=False,
    )
```

```python
import functools

import jax
import jax.numpy as jnp
from jax import lax
from jax.experimental import pallas as pl
from jax.experimental.pallas import tpu as pltpu
from jax.sharding import Mesh
from jax.sharding import PartitionSpec as P

HEADS = 64
KV_HEADS = 8
HEAD_DIM = 128
BLOCK = 128
LOG2E = 1.4426950408889634
CHUNK = 4
GROUP_HEADS = 2
PIECE = 512


def plan_kernel(place_ref, codes_ref, counts_ref, list_ref, fill_ref, *, blocks, sizes, zero):
    x_size, y_size, core_size = sizes
    x, y, core = place_ref[0], place_ref[1], place_ref[2]
    shard = (x * y_size + y) * core_size + core
    for a in range(blocks):
        list_ref[a, 0] = a
        list_ref[blocks + a, 0] = a
        fill_ref[a] = 1

    def visit_shard(slot, _):
        from_x = lax.rem(x + lax.rem(slot, x_size), x_size)
        from_y = lax.rem(y + lax.rem(lax.div(slot, x_size), y_size), y_size)
        from_core = lax.rem(core + lax.div(slot, x_size * y_size), core_size)
        j = (from_x * y_size + from_y) * core_size + from_core

        def visit_entry(c, _):
            code = codes_ref[shard, j, c]
            a = lax.div(code, blocks)
            block = slot * blocks + lax.rem(code, blocks)
            at = fill_ref[a]
            list_ref[a, at] = block
            list_ref[blocks + a, at] = block
            fill_ref[a] = at + 1
            return 0

        return lax.fori_loop(0, counts_ref[shard, j], visit_entry, 0)

    lax.fori_loop(0, x_size * y_size * core_size, visit_shard, 0)
    for a in range(blocks):
        filled = fill_ref[a]
        chunks = lax.div(filled + CHUNK - 1, CHUNK)
        list_ref[2 * blocks, a] = chunks

        def pad(at, _):
            list_ref[a, at] = a
            list_ref[blocks + a, at] = zero
            return 0

        lax.fori_loop(filled, chunks * CHUNK, pad, 0)


def plan(place, live_keys, live_count, blocks, sizes, zero):
    shards = live_keys.shape[0]
    width = -(-(shards * blocks + 1) // CHUNK) * CHUNK
    smem = pl.BlockSpec(memory_space=pltpu.SMEM)
    return pl.pallas_call(
        functools.partial(plan_kernel, blocks=blocks, sizes=sizes, zero=zero),
        in_specs=[smem] * 3,
        out_specs=smem,
        out_shape=jax.ShapeDtypeStruct((2 * blocks + 1, width), jnp.int32),
        scratch_shapes=[pltpu.SMEM((blocks,), jnp.int32)],
        cost_estimate=pl.CostEstimate(flops=0, bytes_accessed=20_000_000, transcendentals=0),
    )(place, live_keys, live_count)


def attend_kernel(listed, queries, *refs, heads, shards):
    pieces, (out, pairs, ones, total, peak, scaled, *rest) = refs[:shards], refs[shards:]
    groups = heads // GROUP_HEADS
    raw, soft, (level, fade, late_fade, ready, sem) = rest[:groups], rest[groups : groups + 2], rest[groups + 2 :]
    b, blocks = pl.program_id(0), pl.num_programs(0)
    count = pairs.shape[0] - 1
    span = count // shards
    width = GROUP_HEADS * BLOCK
    scale = HEAD_DIM**-0.5 * LOG2E

    def arrival(j):
        return pltpu.make_async_copy(pieces[j], pairs.at[pl.ds(j * span, span)], sem.at[j])

    @pl.when(b == 0)
    def _():
        for j in range(shards):
            arrival(j).start()
        ready[0] = 0
        ones[0] = jnp.ones(ones.shape[1:], jnp.bfloat16)
        ones[1] = jnp.zeros(ones.shape[1:], jnp.bfloat16)
        pairs[count] = jnp.zeros(pairs.shape[1:], jnp.bfloat16)

    def arrive(i):
        @pl.when(b == 0)
        def _():
            last = lax.div(listed[b, i * CHUNK + CHUNK - 1], span) + 1
            needed = jnp.where(i >= listed[2 * blocks, b] - 1, shards, last)
            for j in range(shards):

                @pl.when((j >= ready[0]) & (j < needed))
                def _():
                    arrival(j).wait()

            ready[0] = jnp.maximum(ready[0], needed)

    def keys_of(i):
        return jnp.concatenate(
            [pairs[listed[b, i * CHUNK + c], :, :HEAD_DIM] for c in range(CHUNK)], axis=0
        )

    def values_of(i):
        slots = [listed[blocks + b, i * CHUNK + c] for c in range(CHUNK)]
        return jnp.concatenate(
            [
                jnp.concatenate([pairs[s, :, HEAD_DIM:] for s in slots], axis=1),
                jnp.concatenate([ones[(s == count).astype(jnp.int32)] for s in slots], axis=1),
            ],
            axis=0,
        )

    cuts = [slice(j * PIECE, (j + 1) * PIECE) for j in range(CHUNK * BLOCK // PIECE)]

    def columns(g):
        return slice(g * width, (g + 1) * width)

    def score(keys, g):
        return lax.dot_general(
            jnp.concatenate([keys, keys], axis=1),
            scaled[columns(g), :],
            (((1,), (1,)), ((), ())),
            preferred_element_type=jnp.float32,
        )

    def partial_max(piece):
        return jnp.max(piece.reshape(-1, 8, width), axis=0)

    for h in range(heads):
        at = slice(h * BLOCK, (h + 1) * BLOCK)
        exact = queries[:, h * HEAD_DIM : (h + 1) * HEAD_DIM].astype(jnp.float32) * scale
        high = exact.astype(jnp.bfloat16)
        scaled[at, :HEAD_DIM] = high
        scaled[at, HEAD_DIM:] = (exact - high.astype(jnp.float32)).astype(jnp.bfloat16)
    total[...] = jnp.zeros(total.shape, jnp.float32)
    peak[...] = jnp.full(peak.shape, -jnp.inf, jnp.float32)
    soft[1][...] = jnp.zeros(soft[1].shape, jnp.bfloat16)
    late_fade[...] = jnp.ones(late_fade.shape, jnp.float32)
    arrive(0)
    keys = keys_of(0)
    for g in range(2):
        raw[g][...] = score(keys, g)
    level[...] = jnp.max(partial_max(raw[0][...]), axis=0, keepdims=True)
    peak[:, columns(0)] = level[...]
    fade[...] = jnp.zeros(fade.shape, jnp.float32)
    end = listed[2 * blocks, b]

    def visit(i, _):
        following = jnp.minimum(i + 1, end - 1)
        arrive(following)
        keys = keys_of(i)
        next_keys = keys_of(following)
        values = values_of(i)
        before = values_of(jnp.maximum(i - 1, 0))
        new, factor, late = level[...], fade[...], late_fade[...]
        for g in range(groups):
            ahead, upcoming, done = (g + 2) % groups, (g + 1) % groups, (g - 1) % groups
            source = keys if g + 2 < groups else next_keys
            multiplier = values if g else before
            into = columns(done)
            total[:, into] = total[:, into] * late
            tops = None
            for cut in cuts:
                raw[ahead][cut, :] = score(source[cut, :], ahead)
                soft[g % 2][cut, :] = jnp.exp2(raw[g][cut, :] - new).astype(jnp.bfloat16)
                total[:, into] += jnp.dot(
                    multiplier[:, cut], soft[(g + 1) % 2][cut, :], preferred_element_type=jnp.float32
                )
                most = partial_max(raw[upcoming][cut, :])
                tops = most if tops is None else jnp.maximum(tops, most)
            at = columns(upcoming)
            old = peak[:, at]
            new = jnp.maximum(old, jnp.max(tops, axis=0, keepdims=True))
            peak[:, at] = new
            factor, late = jnp.exp2(old - new), factor
        level[...] = new
        fade[...] = factor
        late_fade[...] = late
        return 0

    lax.fori_loop(0, end, visit, 0)
    at = columns(groups - 1)
    total[:, at] = total[:, at] * late_fade[...] + jnp.dot(
        values_of(end - 1), soft[1][...], preferred_element_type=jnp.float32
    )
    square = (BLOCK, BLOCK)
    unit = (
        lax.broadcasted_iota(jnp.int32, square, 0) == lax.broadcasted_iota(jnp.int32, square, 1)
    ).astype(jnp.bfloat16)
    for h in range(heads):
        at = slice(h * BLOCK, (h + 1) * BLOCK)
        normed = (total[:HEAD_DIM, at] / total[HEAD_DIM : HEAD_DIM + 1, at]).astype(jnp.bfloat16)
        turned = lax.dot_general(
            unit, normed, (((1,), (1,)), ((), ())), preferred_element_type=jnp.float32
        )
        out[:, h * HEAD_DIM : (h + 1) * HEAD_DIM] = turned.astype(jnp.bfloat16)


def attend(queries, pieces, lists):
    rows, width = queries.shape
    heads = width // HEAD_DIM
    shards = len(pieces)
    span = pieces[0].shape[0] // BLOCK
    count = shards * span
    pieces = [pltpu.with_memory_space_constraint(piece.reshape(span, BLOCK, -1), pltpu.HBM) for piece in pieces]
    pair_estimate = 180 * 2 * 2 * heads * BLOCK * BLOCK * HEAD_DIM
    return pl.pallas_call(
        functools.partial(attend_kernel, heads=heads, shards=shards),
        grid_spec=pltpu.PrefetchScalarGridSpec(
            num_scalar_prefetch=1,
            grid=(rows // BLOCK,),
            in_specs=[pl.BlockSpec((BLOCK, width), lambda b, *_: (b, 0))]
            + [pl.BlockSpec(memory_space=pl.ANY)] * shards,
            out_specs=pl.BlockSpec((BLOCK, width), lambda b, *_: (b, 0)),
            scratch_shapes=[
                pltpu.VMEM((count + 1, BLOCK, 2 * HEAD_DIM), jnp.bfloat16),
                pltpu.VMEM((2, 16, BLOCK), jnp.bfloat16),
                pltpu.VMEM((HEAD_DIM + 16, heads * BLOCK), jnp.float32),
                pltpu.VMEM((1, heads * BLOCK), jnp.float32),
                pltpu.VMEM((heads * BLOCK, 2 * HEAD_DIM), jnp.bfloat16),
            ]
            + [pltpu.VMEM((CHUNK * BLOCK, GROUP_HEADS * BLOCK), jnp.float32)] * (heads // GROUP_HEADS)
            + [pltpu.VMEM((CHUNK * BLOCK, GROUP_HEADS * BLOCK), jnp.bfloat16)] * 2
            + [pltpu.VMEM((1, GROUP_HEADS * BLOCK), jnp.float32)] * 3
            + [
                pltpu.SMEM((1,), jnp.int32),
                pltpu.SemaphoreType.DMA((shards,)),
            ],
        ),
        out_shape=jax.ShapeDtypeStruct((rows, width), jnp.bfloat16),
        compiler_params=pltpu.CompilerParams(vmem_limit_bytes=48 * 1024 * 1024),
        cost_estimate=pl.CostEstimate(flops=pair_estimate * 3, bytes_accessed=12_000_000, transcendentals=0),
    )(lists, queries, *pieces)


def shift(array, axis, step):
    size = lax.axis_size(axis)
    return lax.ppermute(array, axis, [(i, (i + step) % size) for i in range(size)])


def gather_shards(own):
    across = shift(own, "y_lo", 1)
    here = [own, shift(own, "x", -1), None, shift(own, "x", 1)]
    here[2] = shift(here[3], "x", 1)
    there = [across, shift(across, "x", -1), None, shift(across, "x", 1)]
    there[2] = shift(there[1], "x", -1)
    near = here + there
    return near + [shift(piece, "core", 1) for piece in near]


def local(queries, keys, values, live_keys, live_count):
    head_axes, blk_axes = ("y_hi", "z"), ("x", "y_lo", "core")
    parts = lax.axis_size(head_axes)
    tokens = queries.shape[0]
    sizes = tuple(lax.axis_size(axis) for axis in blk_axes)
    blocks = parts * tokens // BLOCK

    def exchange(cut):
        moved = lax.all_to_all(cut, head_axes, split_axis=0, concat_axis=0, tiled=True)
        return moved.reshape(parts * tokens, -1)

    def cut(array):
        return array.reshape(tokens, parts, -1)

    own = exchange(
        jnp.concatenate([cut(keys).transpose(1, 0, 2), cut(values).transpose(1, 2, 0)], axis=2)
    )
    place = jnp.stack([lax.axis_index(axis) for axis in blk_axes]).astype(jnp.int32)
    lists = plan(place, live_keys, live_count, blocks, sizes, live_keys.shape[0] * blocks)
    own, lists, query_parts = lax.optimization_barrier((own, lists, cut(queries).transpose(1, 0, 2)))
    pieces = gather_shards(own)
    attended = attend(exchange(query_parts), pieces, lists)
    back = lax.all_to_all(
        attended.reshape(parts, tokens, -1), head_axes, split_axis=0, concat_axis=0, tiled=True
    )
    return back.transpose(1, 0, 2).reshape(tokens, -1)


def solution(mesh):
    fine = Mesh(mesh.devices.reshape(4, 2, 2, 2, 4), ("x", "y_lo", "core", "y_hi", "z"))
    rows = P(("x", "y_lo", "core", "y_hi", "z"), None)
    return jax.shard_map(
        local,
        mesh=fine,
        in_specs=(rows, rows, rows, P(), P()),
        out_specs=rows,
        check_vma=False,
    )
```

```python
import functools

import jax
import jax.numpy as jnp
from jax import lax
from jax.experimental import pallas as pl
from jax.experimental.pallas import tpu as pltpu
from jax.sharding import Mesh
from jax.sharding import PartitionSpec as P

HEADS = 64
KV_HEADS = 8
HEAD_DIM = 128
BLOCK = 128
LOG2E = 1.4426950408889634
CHUNK = 4
GROUP_HEADS = 2
PIECE = 512
WAVE = 4


def plan_kernel(place_ref, codes_ref, counts_ref, list_ref, fill_ref, *, blocks, sizes, zero):
    x_size, y_size, core_size = sizes
    x, y, core = place_ref[0], place_ref[1], place_ref[2]
    shard = (x * y_size + y) * core_size + core
    for a in range(blocks):
        list_ref[a, 0] = a
        list_ref[blocks + a, 0] = a
        fill_ref[a] = 1

    def visit_shard(slot, _):
        from_x = lax.rem(x + lax.rem(slot, x_size), x_size)
        from_y = lax.rem(y + lax.rem(lax.div(slot, x_size), y_size), y_size)
        from_core = lax.rem(core + lax.div(slot, x_size * y_size), core_size)
        j = (from_x * y_size + from_y) * core_size + from_core

        def visit_entry(c, _):
            code = codes_ref[shard, j, c]
            a = lax.div(code, blocks)
            block = slot * blocks + lax.rem(code, blocks)
            at = fill_ref[a]
            list_ref[a, at] = block
            list_ref[blocks + a, at] = block
            fill_ref[a] = at + 1
            return 0

        return lax.fori_loop(0, counts_ref[shard, j], visit_entry, 0)

    lax.fori_loop(0, x_size * y_size * core_size, visit_shard, 0)
    for a in range(blocks):
        filled = fill_ref[a]
        chunks = lax.div(filled + CHUNK - 1, CHUNK)
        list_ref[2 * blocks, a] = chunks

        def pad(at, _):
            list_ref[a, at] = a
            list_ref[blocks + a, at] = zero
            return 0

        lax.fori_loop(filled, chunks * CHUNK, pad, 0)


def plan(place, live_keys, live_count, blocks, sizes, zero):
    shards = live_keys.shape[0]
    width = -(-(shards * blocks + 1) // CHUNK) * CHUNK
    smem = pl.BlockSpec(memory_space=pltpu.SMEM)
    return pl.pallas_call(
        functools.partial(plan_kernel, blocks=blocks, sizes=sizes, zero=zero),
        in_specs=[smem] * 3,
        out_specs=smem,
        out_shape=jax.ShapeDtypeStruct((2 * blocks + 1, width), jnp.int32),
        scratch_shapes=[pltpu.SMEM((blocks,), jnp.int32)],
        cost_estimate=pl.CostEstimate(flops=0, bytes_accessed=20_000_000, transcendentals=0),
    )(place, live_keys, live_count)


def attend_kernel(listed, queries, *refs, heads, shards):
    pieces, (out, pairs, ones, total, peak, *rest) = refs[:shards], refs[shards:]
    groups = heads // GROUP_HEADS
    raw, soft, (level, fade, late_fade, ready, sem) = rest[:groups], rest[groups : groups + 2], rest[groups + 2 :]
    b, blocks = pl.program_id(0), pl.num_programs(0)
    count = pairs.shape[0] - 1
    span = count // shards
    width = GROUP_HEADS * BLOCK
    scale = HEAD_DIM**-0.5 * LOG2E

    def arrival(j):
        return pltpu.make_async_copy(pieces[j], pairs.at[pl.ds(j * span, span)], sem.at[j])

    @pl.when(b == 0)
    def _():
        for j in range(WAVE):
            arrival(j).start()
        ready[0] = 0
        ones[0] = jnp.ones(ones.shape[1:], jnp.bfloat16)
        ones[1] = jnp.zeros(ones.shape[1:], jnp.bfloat16)
        pairs[count] = jnp.zeros(pairs.shape[1:], jnp.bfloat16)

    def arrive(i):
        @pl.when(b == 0)
        def _():
            last = lax.div(listed[b, i * CHUNK + CHUNK - 1], span) + 1
            needed = jnp.where(i >= listed[2 * blocks, b] - 1, shards, last)
            for j in range(shards):

                @pl.when((j >= ready[0]) & (j < needed))
                def _():
                    arrival(j).wait()
                    if j + WAVE < shards:
                        arrival(j + WAVE).start()

            ready[0] = jnp.maximum(ready[0], needed)

    def keys_of(i):
        return jnp.concatenate(
            [pairs[listed[b, i * CHUNK + c], :, :HEAD_DIM] for c in range(CHUNK)], axis=0
        )

    def values_of(i):
        slots = [listed[blocks + b, i * CHUNK + c] for c in range(CHUNK)]
        return jnp.concatenate(
            [
                jnp.concatenate([pairs[s, :, HEAD_DIM:] for s in slots], axis=1),
                jnp.concatenate([ones[(s == count).astype(jnp.int32)] for s in slots], axis=1),
            ],
            axis=0,
        )

    cuts = [slice(j * PIECE, (j + 1) * PIECE) for j in range(CHUNK * BLOCK // PIECE)]

    def columns(g):
        return slice(g * width, (g + 1) * width)

    def score(keys, g):
        first = g * GROUP_HEADS
        tile = jnp.concatenate(
            [queries[:, h * HEAD_DIM : (h + 1) * HEAD_DIM] for h in range(first, first + GROUP_HEADS)], axis=0
        )
        return lax.dot_general(keys, tile, (((1,), (1,)), ((), ())), preferred_element_type=jnp.float32)

    def partial_max(piece):
        return jnp.max(piece.reshape(-1, 8, width), axis=0)

    total[...] = jnp.zeros(total.shape, jnp.float32)
    peak[...] = jnp.full(peak.shape, -jnp.inf, jnp.float32)
    soft[1][...] = jnp.zeros(soft[1].shape, jnp.bfloat16)
    late_fade[...] = jnp.ones(late_fade.shape, jnp.float32)
    arrive(0)
    keys = keys_of(0)
    for g in range(2):
        raw[g][...] = score(keys, g)
    level[...] = jnp.max(partial_max(raw[0][...]), axis=0, keepdims=True) * scale
    peak[:, columns(0)] = level[...]
    fade[...] = jnp.zeros(fade.shape, jnp.float32)
    end = listed[2 * blocks, b]

    def visit(i, _):
        following = jnp.minimum(i + 1, end - 1)
        arrive(following)
        keys = keys_of(i)
        next_keys = keys_of(following)
        values = values_of(i)
        before = values_of(jnp.maximum(i - 1, 0))
        new, factor, late = level[...], fade[...], late_fade[...]
        for g in range(groups):
            ahead, upcoming, done = (g + 2) % groups, (g + 1) % groups, (g - 1) % groups
            source = keys if g + 2 < groups else next_keys
            multiplier = values if g else before
            into = columns(done)
            total[:, into] = total[:, into] * late
            tops = None
            for cut in cuts:
                raw[ahead][cut, :] = score(source[cut, :], ahead)
                soft[g % 2][cut, :] = jnp.exp2(raw[g][cut, :] * scale - new).astype(jnp.bfloat16)
                total[:, into] += jnp.dot(
                    multiplier[:, cut], soft[(g + 1) % 2][cut, :], preferred_element_type=jnp.float32
                )
                most = partial_max(raw[upcoming][cut, :])
                tops = most if tops is None else jnp.maximum(tops, most)
            at = columns(upcoming)
            old = peak[:, at]
            new = jnp.maximum(old, jnp.max(tops, axis=0, keepdims=True) * scale)
            peak[:, at] = new
            factor, late = jnp.exp2(old - new), factor
        level[...] = new
        fade[...] = factor
        late_fade[...] = late
        return 0

    lax.fori_loop(0, end, visit, 0)
    at = columns(groups - 1)
    total[:, at] = total[:, at] * late_fade[...] + jnp.dot(
        values_of(end - 1), soft[1][...], preferred_element_type=jnp.float32
    )
    square = (BLOCK, BLOCK)
    unit = (
        lax.broadcasted_iota(jnp.int32, square, 0) == lax.broadcasted_iota(jnp.int32, square, 1)
    ).astype(jnp.bfloat16)
    for h in range(heads):
        at = slice(h * BLOCK, (h + 1) * BLOCK)
        normed = (total[:HEAD_DIM, at] / total[HEAD_DIM : HEAD_DIM + 1, at]).astype(jnp.bfloat16)
        turned = lax.dot_general(
            unit, normed, (((1,), (1,)), ((), ())), preferred_element_type=jnp.float32
        )
        out[:, h * HEAD_DIM : (h + 1) * HEAD_DIM] = turned.astype(jnp.bfloat16)


def attend(queries, pieces, lists):
    rows, width = queries.shape
    heads = width // HEAD_DIM
    shards = len(pieces)
    span = pieces[0].shape[0] // BLOCK
    count = shards * span
    pieces = [pltpu.with_memory_space_constraint(piece.reshape(span, BLOCK, -1), pltpu.HBM) for piece in pieces]
    pair_estimate = 180 * 2 * 2 * heads * BLOCK * BLOCK * HEAD_DIM
    return pl.pallas_call(
        functools.partial(attend_kernel, heads=heads, shards=shards),
        grid_spec=pltpu.PrefetchScalarGridSpec(
            num_scalar_prefetch=1,
            grid=(rows // BLOCK,),
            in_specs=[pl.BlockSpec((BLOCK, width), lambda b, *_: (b, 0))]
            + [pl.BlockSpec(memory_space=pl.ANY)] * shards,
            out_specs=pl.BlockSpec((BLOCK, width), lambda b, *_: (b, 0)),
            scratch_shapes=[
                pltpu.VMEM((count + 1, BLOCK, 2 * HEAD_DIM), jnp.bfloat16),
                pltpu.VMEM((2, 16, BLOCK), jnp.bfloat16),
                pltpu.VMEM((HEAD_DIM + 16, heads * BLOCK), jnp.float32),
                pltpu.VMEM((1, heads * BLOCK), jnp.float32),
            ]
            + [pltpu.VMEM((CHUNK * BLOCK, GROUP_HEADS * BLOCK), jnp.float32)] * (heads // GROUP_HEADS)
            + [pltpu.VMEM((CHUNK * BLOCK, GROUP_HEADS * BLOCK), jnp.bfloat16)] * 2
            + [pltpu.VMEM((1, GROUP_HEADS * BLOCK), jnp.float32)] * 3
            + [
                pltpu.SMEM((1,), jnp.int32),
                pltpu.SemaphoreType.DMA((shards,)),
            ],
        ),
        out_shape=jax.ShapeDtypeStruct((rows, width), jnp.bfloat16),
        compiler_params=pltpu.CompilerParams(vmem_limit_bytes=48 * 1024 * 1024),
        cost_estimate=pl.CostEstimate(flops=pair_estimate * 3, bytes_accessed=12_000_000, transcendentals=0),
    )(lists, queries, *pieces)


def shift(array, axis, step):
    size = lax.axis_size(axis)
    return lax.ppermute(array, axis, [(i, (i + step) % size) for i in range(size)])


def gather_shards(own):
    across = shift(own, "y_lo", 1)
    up, down = shift(own, "x", -1), shift(own, "x", 1)
    across, up, down = lax.optimization_barrier((across, up, down))
    here = [own, up, None, down]
    here[2] = shift(here[3], "x", 1)
    there = [across, shift(across, "x", -1), None, shift(across, "x", 1)]
    there[2] = shift(there[1], "x", -1)
    near = here + there
    return near + [shift(piece, "core", 1) for piece in near]


def local(queries, keys, values, live_keys, live_count):
    head_axes, blk_axes = ("y_hi", "z"), ("x", "y_lo", "core")
    parts = lax.axis_size(head_axes)
    tokens = queries.shape[0]
    sizes = tuple(lax.axis_size(axis) for axis in blk_axes)
    blocks = parts * tokens // BLOCK

    def exchange(cut):
        moved = lax.all_to_all(cut, head_axes, split_axis=0, concat_axis=0, tiled=True)
        return moved.reshape(parts * tokens, -1)

    def cut(array):
        return array.reshape(tokens, parts, -1)

    own = exchange(
        jnp.concatenate([cut(keys).transpose(1, 0, 2), cut(values).transpose(1, 2, 0)], axis=2)
    )
    place = jnp.stack([lax.axis_index(axis) for axis in blk_axes]).astype(jnp.int32)
    lists = plan(place, live_keys, live_count, blocks, sizes, live_keys.shape[0] * blocks)
    own, lists, query_parts = lax.optimization_barrier((own, lists, cut(queries).transpose(1, 0, 2)))
    pieces = gather_shards(own)
    attended = attend(exchange(query_parts), pieces, lists)
    back = lax.all_to_all(
        attended.reshape(parts, tokens, -1), head_axes, split_axis=0, concat_axis=0, tiled=True
    )
    return back.transpose(1, 0, 2).reshape(tokens, -1)


def solution(mesh):
    fine = Mesh(mesh.devices.reshape(4, 2, 2, 2, 4), ("x", "y_lo", "core", "y_hi", "z"))
    rows = P(("x", "y_lo", "core", "y_hi", "z"), None)
    return jax.shard_map(
        local,
        mesh=fine,
        in_specs=(rows, rows, rows, P(), P()),
        out_specs=rows,
        check_vma=False,
    )
```

```python
import functools

import jax
import jax.numpy as jnp
from jax import lax
from jax.experimental import pallas as pl
from jax.experimental.pallas import tpu as pltpu
from jax.sharding import Mesh
from jax.sharding import PartitionSpec as P

HEADS = 64
KV_HEADS = 8
HEAD_DIM = 128
BLOCK = 128
LOG2E = 1.4426950408889634
CHUNK = 4
GROUP_HEADS = 2
PIECE = 512
WAVE = 8
FIRST_STEPS = 5


def plan_kernel(place_ref, codes_ref, counts_ref, list_ref, fill_ref, *, blocks, sizes, zero, far):
    x_size, y_lo_size, core_size = sizes[:3]
    x, y, core = place_ref[0], place_ref[1], place_ref[2]
    shard = (x * y_lo_size + y) * core_size + core
    for a in range(blocks):
        list_ref[a, 0] = a
        list_ref[blocks + a, 0] = a
        fill_ref[a] = 1

    y_hi, z = place_ref[3], place_ref[4]
    y_size, z_size = sizes[3:]
    for step, (dy, dz) in enumerate(far):
        for row, sign in ((1, 1), (2, -1)):
            to_y = lax.rem(y_hi + sign * dy + y_size, y_size)
            to_z = lax.rem(z + sign * dz + z_size, z_size)
            list_ref[2 * blocks + row, step] = to_y * z_size + to_z

    def visit_shard(slot, _):
        from_x = lax.rem(x + lax.rem(slot, x_size), x_size)
        from_y = lax.rem(y + lax.rem(lax.div(slot, x_size), y_lo_size), y_lo_size)
        from_core = lax.rem(core + lax.div(slot, x_size * y_lo_size), core_size)
        j = (from_x * y_lo_size + from_y) * core_size + from_core

        def visit_entry(c, _):
            code = codes_ref[shard, j, c]
            a = lax.div(code, blocks)
            block = slot * blocks + lax.rem(code, blocks)
            at = fill_ref[a]
            list_ref[a, at] = block
            list_ref[blocks + a, at] = block
            fill_ref[a] = at + 1
            return 0

        return lax.fori_loop(0, counts_ref[shard, j], visit_entry, 0)

    lax.fori_loop(0, x_size * y_lo_size * core_size, visit_shard, 0)
    for a in range(blocks):
        filled = fill_ref[a]
        chunks = lax.div(filled + CHUNK - 1, CHUNK)
        list_ref[2 * blocks, a] = chunks

        def pad(at, _):
            list_ref[a, at] = a
            list_ref[blocks + a, at] = zero
            return 0

        lax.fori_loop(filled, chunks * CHUNK, pad, 0)


def plan(place, live_keys, live_count, blocks, sizes, zero, far):
    shards = live_keys.shape[0]
    width = -(-(shards * blocks + 1) // CHUNK) * CHUNK
    smem = pl.BlockSpec(memory_space=pltpu.SMEM)
    return pl.pallas_call(
        functools.partial(plan_kernel, blocks=blocks, sizes=sizes, zero=zero, far=far),
        in_specs=[smem] * 3,
        out_specs=smem,
        out_shape=jax.ShapeDtypeStruct((2 * blocks + 3, width), jnp.int32),
        scratch_shapes=[pltpu.SMEM((blocks,), jnp.int32)],
        cost_estimate=pl.CostEstimate(flops=0, bytes_accessed=20_000_000, transcendentals=0),
    )(place, live_keys, live_count)


def attend_kernel(listed, queries, *refs, blocks, steps, heads, shards, loads):
    if loads:
        pieces, (out, pairs, *rest) = refs[:shards], refs[shards:]
    else:
        pairs, out, *rest = refs
    ones, total, peak, *rest = rest
    groups = heads // GROUP_HEADS
    raw, soft, (level, fade, late_fade, *loading) = rest[:groups], rest[groups : groups + 2], rest[groups + 2 :]
    count = pairs.shape[0] - 1
    span = count // shards
    width = GROUP_HEADS * BLOCK
    scale = HEAD_DIM**-0.5 * LOG2E
    cuts = [slice(j * PIECE, (j + 1) * PIECE) for j in range(CHUNK * BLOCK // PIECE)]
    square = (BLOCK, BLOCK)
    unit = (
        lax.broadcasted_iota(jnp.int32, square, 0) == lax.broadcasted_iota(jnp.int32, square, 1)
    ).astype(jnp.bfloat16)

    def block_of(step):
        return listed[2 * blocks + 1, step]

    def arrival(j):
        return pltpu.make_async_copy(pieces[j], pairs.at[pl.ds(j * span, span)], loading[1].at[j])

    def arrive(b, i):
        ready = loading[0]
        last = lax.div(listed[b, i * CHUNK + CHUNK - 1], span) + 1
        needed = jnp.where(i >= listed[2 * blocks, b] - 1, shards, last)
        for j in range(shards):

            @pl.when((j >= ready[0]) & (j < needed))
            def _():
                arrival(j).wait()
                if j + WAVE < shards:
                    arrival(j + WAVE).start()

        ready[0] = jnp.maximum(ready[0], needed)

    def rows_of(b):
        return pl.ds(pl.multiple_of(b * BLOCK, BLOCK), BLOCK)

    def columns(g):
        return slice(g * width, (g + 1) * width)

    def keys_of(b, i):
        return jnp.concatenate([pairs[listed[b, i * CHUNK + c], :, :HEAD_DIM] for c in range(CHUNK)], axis=0)

    def values_of(b, i):
        slots = [listed[blocks + b, i * CHUNK + c] for c in range(CHUNK)]
        return jnp.concatenate(
            [
                jnp.concatenate([pairs[s, :, HEAD_DIM:] for s in slots], axis=1),
                jnp.concatenate([ones[(s == count).astype(jnp.int32)] for s in slots], axis=1),
            ],
            axis=0,
        )

    def score(b, keys, g):
        first = g * GROUP_HEADS
        tile = jnp.concatenate(
            [
                queries[rows_of(b), h * HEAD_DIM : (h + 1) * HEAD_DIM]
                for h in range(first, first + GROUP_HEADS)
            ],
            axis=0,
        )
        return lax.dot_general(keys, tile, (((1,), (1,)), ((), ())), preferred_element_type=jnp.float32)

    def partial_max(piece):
        return jnp.max(piece.reshape(-1, 8, width), axis=0)

    def first_scores(b):
        keys = keys_of(b, 0)
        for g in range(2):
            raw[g][...] = score(b, keys, g)

    def reset():
        total[...] = jnp.zeros(total.shape, jnp.float32)
        peak[...] = jnp.full(peak.shape, -jnp.inf, jnp.float32)
        soft[1][...] = jnp.zeros(soft[1].shape, jnp.bfloat16)
        late_fade[...] = jnp.ones(late_fade.shape, jnp.float32)
        level[...] = jnp.max(partial_max(raw[0][...]), axis=0, keepdims=True) * scale
        peak[:, columns(0)] = level[...]
        fade[...] = jnp.zeros(fade.shape, jnp.float32)

    ones[0] = jnp.ones(ones.shape[1:], jnp.bfloat16)
    ones[1] = jnp.zeros(ones.shape[1:], jnp.bfloat16)
    if loads:
        for j in range(WAVE):
            arrival(j).start()
        loading[0][0] = 0
        pairs[count] = jnp.zeros(pairs.shape[1:], jnp.bfloat16)
        arrive(block_of(steps[0]), 0)
    first_scores(block_of(steps[0]))
    reset()

    def visit_block(step, _):
        b = block_of(step)
        end = listed[2 * blocks, b]

        def visit(i, _):
            following = jnp.minimum(i + 1, end - 1)

            if loads:

                @pl.when(step == steps[0])
                def _():
                    arrive(b, following)

            keys = keys_of(b, i)
            next_keys = keys_of(b, following)
            values = values_of(b, i)
            before = values_of(b, jnp.maximum(i - 1, 0))
            new, factor, late = level[...], fade[...], late_fade[...]
            for g in range(groups):
                ahead, upcoming, done = (g + 2) % groups, (g + 1) % groups, (g - 1) % groups
                source = keys if g + 2 < groups else next_keys
                multiplier = values if g else before
                into = columns(done)
                total[:, into] = total[:, into] * late
                tops = None
                for cut in cuts:
                    raw[ahead][cut, :] = score(b, source[cut, :], ahead)
                    soft[g % 2][cut, :] = jnp.exp2(raw[g][cut, :] * scale - new).astype(jnp.bfloat16)
                    total[:, into] += jnp.dot(
                        multiplier[:, cut], soft[(g + 1) % 2][cut, :], preferred_element_type=jnp.float32
                    )
                    most = partial_max(raw[upcoming][cut, :])
                    tops = most if tops is None else jnp.maximum(tops, most)
                at = columns(upcoming)
                old = peak[:, at]
                new = jnp.maximum(old, jnp.max(tops, axis=0, keepdims=True) * scale)
                peak[:, at] = new
                factor, late = jnp.exp2(old - new), factor
            level[...] = new
            fade[...] = factor
            late_fade[...] = late
            return 0

        lax.fori_loop(0, end, visit, 0)
        at = columns(groups - 1)
        total[:, at] = total[:, at] * late_fade[...] + jnp.dot(
            values_of(b, end - 1), soft[1][...], preferred_element_type=jnp.float32
        )
        first_scores(block_of(jnp.minimum(step + 1, steps[1] - 1)))
        for h in range(heads):
            at = slice(h * BLOCK, (h + 1) * BLOCK)
            inverse = 1.0 / total[HEAD_DIM : HEAD_DIM + 1, at]
            normed = (total[:HEAD_DIM, at] * inverse).astype(jnp.bfloat16)
            turned = lax.dot_general(
                unit, normed, (((1,), (1,)), ((), ())), preferred_element_type=jnp.float32
            )
            out[rows_of(step - steps[0]), h * HEAD_DIM : (h + 1) * HEAD_DIM] = turned.astype(jnp.bfloat16)
        reset()
        return 0

    lax.fori_loop(*steps, visit_block, 0)


def attend(queries, sources, lists, steps):
    rows, width = queries.shape
    heads = width // HEAD_DIM
    blocks = rows // BLOCK
    loads = isinstance(sources, list)
    pair_estimate = 22 * (steps[1] - steps[0]) * 2 * 2 * heads * BLOCK * BLOCK * HEAD_DIM
    vmem = pl.BlockSpec(memory_space=pltpu.VMEM)
    out_specs, out_shape = [vmem], [jax.ShapeDtypeStruct(((steps[1] - steps[0]) * BLOCK, width), jnp.bfloat16)]
    if loads:
        shards = len(sources)
        span = sources[0].shape[0] // BLOCK
        count = shards * span
        sources = [
            pltpu.with_memory_space_constraint(piece.reshape(span, BLOCK, -1), pltpu.HBM) for piece in sources
        ]
        in_specs = [pl.BlockSpec(memory_space=pl.ANY)] * shards
        loading = [pltpu.SMEM((1,), jnp.int32), pltpu.SemaphoreType.DMA((shards,))]
        out_specs.append(vmem)
        out_shape.append(jax.ShapeDtypeStruct((count + 1, BLOCK, 2 * HEAD_DIM), jnp.bfloat16))
    else:
        shards = (sources.shape[0] - 1) // blocks
        sources, in_specs, loading = [sources], [vmem], []
    return pl.pallas_call(
        functools.partial(
            attend_kernel, blocks=blocks, steps=steps, heads=heads, shards=shards, loads=loads
        ),
        in_specs=[pl.BlockSpec(memory_space=pltpu.SMEM), vmem, *in_specs],
        out_specs=out_specs,
        scratch_shapes=[
            pltpu.VMEM((2, 16, BLOCK), jnp.bfloat16),
            pltpu.VMEM((HEAD_DIM + 16, heads * BLOCK), jnp.float32),
            pltpu.VMEM((1, heads * BLOCK), jnp.float32),
        ]
        + [pltpu.VMEM((CHUNK * BLOCK, GROUP_HEADS * BLOCK), jnp.float32)] * (heads // GROUP_HEADS)
        + [pltpu.VMEM((CHUNK * BLOCK, GROUP_HEADS * BLOCK), jnp.bfloat16)] * 2
        + [pltpu.VMEM((1, GROUP_HEADS * BLOCK), jnp.float32)] * 3
        + loading,
        out_shape=out_shape,
        compiler_params=pltpu.CompilerParams(vmem_limit_bytes=32 * 1024 * 1024),
        cost_estimate=pl.CostEstimate(flops=pair_estimate * 3, bytes_accessed=6_000_000, transcendentals=0),
    )(lists, queries, *sources)


def assemble_kernel(listed, *refs):
    *parts, out, sem = refs
    width = parts[0].shape[1]
    copies = [
        pltpu.make_async_copy(
            part, out.at[:, pl.ds(pl.multiple_of(listed[2 * len(parts) + 2, r] * width, width), width)], sem.at[r]
        )
        for r, part in enumerate(parts)
    ]
    for copy in copies:
        copy.start()
    for copy in copies:
        copy.wait()


def assemble(lists, parts):
    rows, width = parts[0].shape
    return pl.pallas_call(
        assemble_kernel,
        in_specs=[pl.BlockSpec(memory_space=pltpu.SMEM)] + [pl.BlockSpec(memory_space=pltpu.VMEM)] * len(parts),
        out_specs=pl.BlockSpec(memory_space=pl.ANY),
        out_shape=jax.ShapeDtypeStruct((rows, width * len(parts)), parts[0].dtype),
        scratch_shapes=[pltpu.SemaphoreType.DMA((len(parts),))],
    )(lists, *parts)


def shift(array, axis, step):
    size = lax.axis_size(axis)
    return lax.ppermute(array, axis, [(i, (i + step) % size) for i in range(size)])


def gather_shards(own):
    across = shift(own, "y_lo", 1)
    up, down = shift(own, "x", -1), shift(own, "x", 1)
    across, up, down = lax.optimization_barrier((across, up, down))
    here = [own, up, None, down]
    here[2] = shift(here[3], "x", 1)
    there = [across, shift(across, "x", -1), None, shift(across, "x", 1)]
    there[2] = shift(there[1], "x", -1)
    near = here + there
    return near + [shift(piece, "core", 1) for piece in near]


def local(queries, keys, values, live_keys, live_count):
    head_axes, blk_axes = ("y_hi", "z"), ("x", "y_lo", "core")
    parts = lax.axis_size(head_axes)
    tokens = queries.shape[0]
    sizes = tuple(lax.axis_size(axis) for axis in blk_axes + head_axes)
    blocks = parts * tokens // BLOCK

    def exchange(cut):
        moved = lax.all_to_all(cut, head_axes, split_axis=0, concat_axis=0, tiled=True)
        return moved.reshape(parts * tokens, -1)

    def cut(array):
        return array.reshape(tokens, parts, -1)

    own = exchange(
        jnp.concatenate([cut(keys).transpose(1, 0, 2), cut(values).transpose(1, 2, 0)], axis=2)
    )
    y_size, z_size = (lax.axis_size(axis) for axis in head_axes)
    far = [(dy, dz) for dy in range(y_size) for dz in range(z_size)]
    far.sort(key=lambda d: (d[0] + min(d[1], z_size - d[1]), d[0]), reverse=True)

    def at_distance(y, z, dy, dz):
        return (y + dy) % y_size * z_size + (z + dz) % z_size

    place = jnp.stack([lax.axis_index(axis) for axis in blk_axes + head_axes]).astype(jnp.int32)
    lists = plan(place, live_keys, live_count, blocks, sizes, live_keys.shape[0] * blocks, far)
    own, lists, query_parts = lax.optimization_barrier((own, lists, cut(queries).transpose(1, 0, 2)))
    pieces = gather_shards(own)
    query_local = exchange(query_parts)

    def send(attended, steps):
        sent = []
        for step in range(*steps):
            part = attended[(step - steps[0]) * tokens : (step - steps[0] + 1) * tokens]
            if any(far[step]):
                pairs = [
                    (k, at_distance(k // z_size, k % z_size, *far[step])) for k in range(y_size * z_size)
                ]
                part = lax.ppermute(part, head_axes, pairs)
            sent.append(part)
        return sent

    early, late = (0, FIRST_STEPS), (FIRST_STEPS, parts)
    attended, gathered = attend(query_local, pieces, lists, early)
    received = send(attended, early)
    (attended,) = attend(query_local, gathered, lists, late)
    received += send(attended, late)
    return assemble(lists, received)


def solution(mesh):
    fine = Mesh(mesh.devices.reshape(4, 2, 2, 2, 4), ("x", "y_lo", "core", "y_hi", "z"))
    rows = P(("x", "y_lo", "core", "y_hi", "z"), None)
    return jax.shard_map(
        local,
        mesh=fine,
        in_specs=(rows, rows, rows, P(), P()),
        out_specs=rows,
        check_vma=False,
    )
```

```python
import functools

import jax
import jax.numpy as jnp
from jax import lax
from jax.experimental import pallas as pl
from jax.experimental.pallas import tpu as pltpu
from jax.sharding import Mesh
from jax.sharding import PartitionSpec as P

HEADS = 64
KV_HEADS = 8
HEAD_DIM = 128
BLOCK = 128
LOG2E = 1.4426950408889634
CHUNK = 4
GROUP_HEADS = 2
PIECE = 512
WAVE = 8
FIRST_STEPS = 5


def plan_kernel(place_ref, codes_ref, counts_ref, list_ref, fill_ref, *, blocks, sizes, zero, far):
    x_size, y_lo_size, core_size = sizes[:3]
    x, y, core = place_ref[0], place_ref[1], place_ref[2]
    shard = (x * y_lo_size + y) * core_size + core
    for a in range(blocks):
        list_ref[a, 0] = a
        list_ref[blocks + a, 0] = a
        fill_ref[a] = 1

    y_hi, z = place_ref[3], place_ref[4]
    y_size, z_size = sizes[3:]
    for step, (dy, dz) in enumerate(far):
        for row, sign in ((1, 1), (2, -1)):
            to_y = lax.rem(y_hi + sign * dy + y_size, y_size)
            to_z = lax.rem(z + sign * dz + z_size, z_size)
            list_ref[2 * blocks + row, step] = to_y * z_size + to_z

    def visit_shard(slot, _):
        from_x = lax.rem(x + lax.rem(slot, x_size), x_size)
        from_y = lax.rem(y + lax.rem(lax.div(slot, x_size), y_lo_size), y_lo_size)
        from_core = lax.rem(core + lax.div(slot, x_size * y_lo_size), core_size)
        j = (from_x * y_lo_size + from_y) * core_size + from_core

        def visit_entry(c, _):
            code = codes_ref[shard, j, c]
            a = lax.div(code, blocks)
            block = slot * blocks + lax.rem(code, blocks)
            at = fill_ref[a]
            list_ref[a, at] = block
            list_ref[blocks + a, at] = block
            fill_ref[a] = at + 1
            return 0

        return lax.fori_loop(0, counts_ref[shard, j], visit_entry, 0)

    lax.fori_loop(0, x_size * y_lo_size * core_size, visit_shard, 0)
    for a in range(blocks):
        filled = fill_ref[a]
        chunks = lax.div(filled + CHUNK - 1, CHUNK)
        list_ref[2 * blocks, a] = chunks

        def pad(at, _):
            list_ref[a, at] = a
            list_ref[blocks + a, at] = zero
            return 0

        lax.fori_loop(filled, chunks * CHUNK, pad, 0)


def plan(place, live_keys, live_count, blocks, sizes, zero, far):
    shards = live_keys.shape[0]
    width = -(-(shards * blocks + 1) // CHUNK) * CHUNK
    smem = pl.BlockSpec(memory_space=pltpu.SMEM)
    return pl.pallas_call(
        functools.partial(plan_kernel, blocks=blocks, sizes=sizes, zero=zero, far=far),
        in_specs=[smem] * 3,
        out_specs=smem,
        out_shape=jax.ShapeDtypeStruct((2 * blocks + 3, width), jnp.int32),
        scratch_shapes=[pltpu.SMEM((blocks,), jnp.int32)],
        cost_estimate=pl.CostEstimate(flops=0, bytes_accessed=20_000_000, transcendentals=0),
    )(place, live_keys, live_count)


def attend_kernel(listed, queries, *refs, blocks, steps, heads, shards, loads):
    if loads:
        pieces, (out, pairs, *rest) = refs[:shards], refs[shards:]
    else:
        pairs, out, *rest = refs
    ones, total, peak, *rest = rest
    groups = heads // GROUP_HEADS
    raw, soft, (level, fade, late_fade, *loading) = rest[:groups], rest[groups : groups + 2], rest[groups + 2 :]
    count = pairs.shape[0] - 1
    span = count // shards
    width = GROUP_HEADS * BLOCK
    scale = HEAD_DIM**-0.5 * LOG2E
    cuts = [slice(j * PIECE, (j + 1) * PIECE) for j in range(CHUNK * BLOCK // PIECE)]
    square = (BLOCK, BLOCK)
    unit = (
        lax.broadcasted_iota(jnp.int32, square, 0) == lax.broadcasted_iota(jnp.int32, square, 1)
    ).astype(jnp.bfloat16)

    def block_of(step):
        return listed[2 * blocks + 1, step]

    def arrival(j):
        return pltpu.make_async_copy(pieces[j], pairs.at[pl.ds(j * span, span)], loading[1].at[j])

    def arrive(b, i):
        ready = loading[0]
        last = lax.div(listed[b, i * CHUNK + CHUNK - 1], span) + 1
        needed = jnp.where(i >= listed[2 * blocks, b] - 1, shards, last)
        for j in range(shards):

            @pl.when((j >= ready[0]) & (j < needed))
            def _():
                arrival(j).wait()
                if j + WAVE < shards:
                    arrival(j + WAVE).start()

        ready[0] = jnp.maximum(ready[0], needed)

    def rows_of(b):
        return pl.ds(pl.multiple_of(b * BLOCK, BLOCK), BLOCK)

    def columns(g):
        return slice(g * width, (g + 1) * width)

    def keys_of(b, i):
        return jnp.concatenate([pairs[listed[b, i * CHUNK + c], :, :HEAD_DIM] for c in range(CHUNK)], axis=0)

    def values_of(b, i):
        slots = [listed[blocks + b, i * CHUNK + c] for c in range(CHUNK)]
        return jnp.concatenate(
            [
                jnp.concatenate([pairs[s, :, HEAD_DIM:] for s in slots], axis=1),
                jnp.concatenate([ones[(s == count).astype(jnp.int32)] for s in slots], axis=1),
            ],
            axis=0,
        )

    def score(b, keys, g):
        first = g * GROUP_HEADS
        tile = jnp.concatenate(
            [
                queries[rows_of(b), h * HEAD_DIM : (h + 1) * HEAD_DIM]
                for h in range(first, first + GROUP_HEADS)
            ],
            axis=0,
        )
        return lax.dot_general(keys, tile, (((1,), (1,)), ((), ())), preferred_element_type=jnp.float32)

    def partial_max(piece):
        return jnp.max(piece.reshape(-1, 8, width), axis=0)

    def first_scores(b):
        keys = keys_of(b, 0)
        for g in range(2):
            raw[g][...] = score(b, keys, g)

    def reset():
        total[...] = jnp.zeros(total.shape, jnp.float32)
        peak[...] = jnp.full(peak.shape, -jnp.inf, jnp.float32)
        soft[1][...] = jnp.zeros(soft[1].shape, jnp.bfloat16)
        late_fade[...] = jnp.ones(late_fade.shape, jnp.float32)
        level[...] = jnp.max(partial_max(raw[0][...]), axis=0, keepdims=True) * scale
        peak[:, columns(0)] = level[...]
        fade[...] = jnp.zeros(fade.shape, jnp.float32)

    ones[0] = jnp.ones(ones.shape[1:], jnp.bfloat16)
    ones[1] = jnp.zeros(ones.shape[1:], jnp.bfloat16)
    if loads:
        for j in range(WAVE):
            arrival(j).start()
        loading[0][0] = 0
        pairs[count] = jnp.zeros(pairs.shape[1:], jnp.bfloat16)
        arrive(block_of(steps[0]), 0)
    first_scores(block_of(steps[0]))
    reset()

    def visit_block(step, _):
        b = block_of(step)
        end = listed[2 * blocks, b]

        def visit(i, _):
            following = jnp.minimum(i + 1, end - 1)

            if loads:

                @pl.when(step == steps[0])
                def _():
                    arrive(b, following)

            keys = keys_of(b, i)
            next_keys = keys_of(b, following)
            values = values_of(b, i)
            before = values_of(b, jnp.maximum(i - 1, 0))
            new, factor, late = level[...], fade[...], late_fade[...]
            for g in range(groups):
                ahead, upcoming, done = (g + 2) % groups, (g + 1) % groups, (g - 1) % groups
                source = keys if g + 2 < groups else next_keys
                multiplier = values if g else before
                into = columns(done)
                total[:, into] = total[:, into] * late
                tops = None
                for cut in cuts:
                    raw[ahead][cut, :] = score(b, source[cut, :], ahead)
                    soft[g % 2][cut, :] = jnp.exp2(raw[g][cut, :] * scale - new).astype(jnp.bfloat16)
                    total[:, into] += jnp.dot(
                        multiplier[:, cut], soft[(g + 1) % 2][cut, :], preferred_element_type=jnp.float32
                    )
                    most = partial_max(raw[upcoming][cut, :])
                    tops = most if tops is None else jnp.maximum(tops, most)
                at = columns(upcoming)
                old = peak[:, at]
                new = jnp.maximum(old, jnp.max(tops, axis=0, keepdims=True) * scale)
                peak[:, at] = new
                factor, late = jnp.exp2(old - new), factor
            level[...] = new
            fade[...] = factor
            late_fade[...] = late
            return 0

        lax.fori_loop(0, end, visit, 0)
        at = columns(groups - 1)
        total[:, at] = total[:, at] * late_fade[...] + jnp.dot(
            values_of(b, end - 1), soft[1][...], preferred_element_type=jnp.float32
        )
        first_scores(block_of(jnp.minimum(step + 1, steps[1] - 1)))
        for h in range(heads):
            at = slice(h * BLOCK, (h + 1) * BLOCK)
            inverse = 1.0 / total[HEAD_DIM : HEAD_DIM + 1, at]
            normed = (total[:HEAD_DIM, at] * inverse).astype(jnp.bfloat16)
            turned = lax.dot_general(
                unit, normed, (((1,), (1,)), ((), ())), preferred_element_type=jnp.float32
            )
            out[rows_of(step - steps[0]), h * HEAD_DIM : (h + 1) * HEAD_DIM] = turned.astype(jnp.bfloat16)
        reset()
        return 0

    lax.fori_loop(*steps, visit_block, 0)


def attend(queries, sources, lists, steps):
    rows, width = queries.shape
    heads = width // HEAD_DIM
    blocks = rows // BLOCK
    loads = isinstance(sources, list)
    pair_estimate = 22 * (steps[1] - steps[0]) * 2 * 2 * heads * BLOCK * BLOCK * HEAD_DIM
    vmem = pl.BlockSpec(memory_space=pltpu.VMEM)
    out_specs, out_shape = [vmem], [jax.ShapeDtypeStruct(((steps[1] - steps[0]) * BLOCK, width), jnp.bfloat16)]
    if loads:
        shards = len(sources)
        span = sources[0].shape[0] // BLOCK
        count = shards * span
        sources = [
            pltpu.with_memory_space_constraint(piece.reshape(span, BLOCK, -1), pltpu.HBM) for piece in sources
        ]
        in_specs = [pl.BlockSpec(memory_space=pl.ANY)] * shards
        loading = [pltpu.SMEM((1,), jnp.int32), pltpu.SemaphoreType.DMA((shards,))]
        out_specs.append(vmem)
        out_shape.append(jax.ShapeDtypeStruct((count + 1, BLOCK, 2 * HEAD_DIM), jnp.bfloat16))
    else:
        shards = (sources.shape[0] - 1) // blocks
        sources, in_specs, loading = [sources], [vmem], []
    return pl.pallas_call(
        functools.partial(
            attend_kernel, blocks=blocks, steps=steps, heads=heads, shards=shards, loads=loads
        ),
        in_specs=[pl.BlockSpec(memory_space=pltpu.SMEM), vmem, *in_specs],
        out_specs=out_specs,
        scratch_shapes=[
            pltpu.VMEM((2, 16, BLOCK), jnp.bfloat16),
            pltpu.VMEM((HEAD_DIM + 16, heads * BLOCK), jnp.float32),
            pltpu.VMEM((1, heads * BLOCK), jnp.float32),
        ]
        + [pltpu.VMEM((CHUNK * BLOCK, GROUP_HEADS * BLOCK), jnp.float32)] * (heads // GROUP_HEADS)
        + [pltpu.VMEM((CHUNK * BLOCK, GROUP_HEADS * BLOCK), jnp.bfloat16)] * 2
        + [pltpu.VMEM((1, GROUP_HEADS * BLOCK), jnp.float32)] * 3
        + loading,
        out_shape=out_shape,
        compiler_params=pltpu.CompilerParams(vmem_limit_bytes=32 * 1024 * 1024),
        cost_estimate=pl.CostEstimate(flops=pair_estimate * 3, bytes_accessed=6_000_000, transcendentals=0),
    )(lists, queries, *sources)


def assemble_kernel(listed, *refs):
    *parts, out, sem = refs
    width = parts[0].shape[1]
    copies = [
        pltpu.make_async_copy(
            part, out.at[:, pl.ds(pl.multiple_of(listed[2 * len(parts) + 2, r] * width, width), width)], sem.at[r]
        )
        for r, part in enumerate(parts)
    ]
    for copy in copies:
        copy.start()
    for copy in copies:
        copy.wait()


def assemble(lists, parts):
    rows, width = parts[0].shape
    return pl.pallas_call(
        assemble_kernel,
        in_specs=[pl.BlockSpec(memory_space=pltpu.SMEM)] + [pl.BlockSpec(memory_space=pltpu.VMEM)] * len(parts),
        out_specs=pl.BlockSpec(memory_space=pl.ANY),
        out_shape=jax.ShapeDtypeStruct((rows, width * len(parts)), parts[0].dtype),
        scratch_shapes=[pltpu.SemaphoreType.DMA((len(parts),))],
    )(lists, *parts)


def shift(array, axis, step):
    size = lax.axis_size(axis)
    return lax.ppermute(array, axis, [(i, (i + step) % size) for i in range(size)])


def gather_shards(own):
    across = shift(own, "y_lo", 1)
    up, down = shift(own, "x", -1), shift(own, "x", 1)
    across, up, down = lax.optimization_barrier((across, up, down))
    here = [own, up, None, down]
    here[2] = shift(here[3], "x", 1)
    there = [across, shift(across, "x", -1), None, shift(across, "x", 1)]
    there[2] = shift(there[1], "x", -1)
    near = here + there
    return near + [shift(piece, "core", 1) for piece in near]


def local(queries, keys, values, live_keys, live_count):
    head_axes, blk_axes = ("y_hi", "z"), ("x", "y_lo", "core")
    parts = lax.axis_size(head_axes)
    tokens = queries.shape[0]
    sizes = tuple(lax.axis_size(axis) for axis in blk_axes + head_axes)
    blocks = parts * tokens // BLOCK

    def exchange(cut):
        moved = lax.all_to_all(cut, head_axes, split_axis=0, concat_axis=0, tiled=True)
        return moved.reshape(parts * tokens, -1)

    def cut(array):
        return array.reshape(tokens, parts, -1)

    own = exchange(
        jnp.concatenate([cut(keys).transpose(1, 0, 2), cut(values).transpose(1, 2, 0)], axis=2)
    )
    y_size, z_size = (lax.axis_size(axis) for axis in head_axes)
    far = [(dy, dz) for dy in range(y_size) for dz in range(z_size)]
    far.sort(key=lambda d: (d[0] + min(d[1], z_size - d[1]), d[0]), reverse=True)

    def at_distance(y, z, dy, dz):
        return (y + dy) % y_size * z_size + (z + dz) % z_size

    place = jnp.stack([lax.axis_index(axis) for axis in blk_axes + head_axes]).astype(jnp.int32)
    lists = plan(place, live_keys, live_count, blocks, sizes, live_keys.shape[0] * blocks, far)
    own, lists, query_parts = lax.optimization_barrier((own, lists, cut(queries).transpose(1, 0, 2)))
    pieces = gather_shards(own)
    query_local = exchange(query_parts)

    def send(attended, steps):
        sent = []
        for step in range(*steps):
            part = attended[(step - steps[0]) * tokens : (step - steps[0] + 1) * tokens]
            if any(far[step]):
                pairs = [
                    (k, at_distance(k // z_size, k % z_size, *far[step])) for k in range(y_size * z_size)
                ]
                part = lax.ppermute(part, head_axes, pairs)
            sent.append(part)
        return sent

    early, late = (0, FIRST_STEPS), (FIRST_STEPS, parts)
    attended, gathered = attend(query_local, pieces, lists, early)
    received = send(attended, early)
    (attended,) = attend(query_local, gathered, lists, late)
    attended, received = lax.optimization_barrier((attended, received))
    received += send(attended, late)
    return assemble(lists, received)


def solution(mesh):
    fine = Mesh(mesh.devices.reshape(4, 2, 2, 2, 4), ("x", "y_lo", "core", "y_hi", "z"))
    rows = P(("x", "y_lo", "core", "y_hi", "z"), None)
    return jax.shard_map(
        local,
        mesh=fine,
        in_specs=(rows, rows, rows, P(), P()),
        out_specs=rows,
        check_vma=False,
    )
```

```python
import functools

import jax
import jax.numpy as jnp
from jax import lax
from jax.experimental import pallas as pl
from jax.experimental.pallas import tpu as pltpu
from jax.sharding import Mesh
from jax.sharding import PartitionSpec as P

HEADS = 64
KV_HEADS = 8
HEAD_DIM = 128
BLOCK = 128
LOG2E = 1.4426950408889634
CHUNK = 4
GROUP_HEADS = 2
PIECE = 512
WAVE = 8
FIRST_STEPS = 5


def pack_kernel(keys, values, out):
    for h in range(out.shape[0]):
        at = slice(h * HEAD_DIM, (h + 1) * HEAD_DIM)
        out[h, :, :HEAD_DIM] = keys[:, at]
        out[h, :, HEAD_DIM:] = values[:, at].T


def pack(keys, values, parts):
    tokens = keys.shape[0]
    vmem = pl.BlockSpec(memory_space=pltpu.VMEM)
    return pl.pallas_call(
        pack_kernel,
        in_specs=[vmem, vmem],
        out_specs=vmem,
        out_shape=jax.ShapeDtypeStruct((parts, tokens, 2 * HEAD_DIM), keys.dtype),
    )(keys, values)


def plan_kernel(place_ref, codes_ref, counts_ref, list_ref, fill_ref, *, blocks, sizes, zero, far):
    x_size, y_lo_size, core_size = sizes[:3]
    x, y, core = place_ref[0], place_ref[1], place_ref[2]
    shard = (x * y_lo_size + y) * core_size + core
    for a in range(blocks):
        list_ref[a, 0] = a
        list_ref[blocks + a, 0] = a
        fill_ref[a] = 1

    y_hi, z = place_ref[3], place_ref[4]
    y_size, z_size = sizes[3:]
    for step, (dy, dz) in enumerate(far):
        for row, sign in ((1, 1), (2, -1)):
            to_y = lax.rem(y_hi + sign * dy + y_size, y_size)
            to_z = lax.rem(z + sign * dz + z_size, z_size)
            list_ref[2 * blocks + row, step] = to_y * z_size + to_z

    def visit_shard(slot, _):
        from_x = lax.rem(x + lax.rem(slot, x_size), x_size)
        from_y = lax.rem(y + lax.rem(lax.div(slot, x_size), y_lo_size), y_lo_size)
        from_core = lax.rem(core + lax.div(slot, x_size * y_lo_size), core_size)
        j = (from_x * y_lo_size + from_y) * core_size + from_core

        def visit_entry(c, _):
            code = codes_ref[shard, j, c]
            a = lax.div(code, blocks)
            block = slot * blocks + lax.rem(code, blocks)
            at = fill_ref[a]
            list_ref[a, at] = block
            list_ref[blocks + a, at] = block
            fill_ref[a] = at + 1
            return 0

        return lax.fori_loop(0, counts_ref[shard, j], visit_entry, 0)

    lax.fori_loop(0, x_size * y_lo_size * core_size, visit_shard, 0)
    for a in range(blocks):
        filled = fill_ref[a]
        chunks = lax.div(filled + CHUNK - 1, CHUNK)
        list_ref[2 * blocks, a] = chunks

        def pad(at, _):
            list_ref[a, at] = a
            list_ref[blocks + a, at] = zero
            return 0

        lax.fori_loop(filled, chunks * CHUNK, pad, 0)


def plan(place, live_keys, live_count, blocks, sizes, zero, far):
    shards = live_keys.shape[0]
    width = -(-(shards * blocks + 1) // CHUNK) * CHUNK
    smem = pl.BlockSpec(memory_space=pltpu.SMEM)
    return pl.pallas_call(
        functools.partial(plan_kernel, blocks=blocks, sizes=sizes, zero=zero, far=far),
        in_specs=[smem] * 3,
        out_specs=smem,
        out_shape=jax.ShapeDtypeStruct((2 * blocks + 3, width), jnp.int32),
        scratch_shapes=[pltpu.SMEM((blocks,), jnp.int32)],
        cost_estimate=pl.CostEstimate(flops=0, bytes_accessed=20_000_000, transcendentals=0),
    )(place, live_keys, live_count)


def attend_kernel(listed, queries, *refs, blocks, steps, heads, shards, loads):
    if loads:
        pieces, (out, pairs, *rest) = refs[:shards], refs[shards:]
    else:
        pairs, out, *rest = refs
    ones, total, peak, *rest = rest
    groups = heads // GROUP_HEADS
    raw, soft, (level, fade, late_fade, *loading) = rest[:groups], rest[groups : groups + 2], rest[groups + 2 :]
    count = pairs.shape[0] - 1
    span = count // shards
    width = GROUP_HEADS * BLOCK
    scale = HEAD_DIM**-0.5 * LOG2E
    cuts = [slice(j * PIECE, (j + 1) * PIECE) for j in range(CHUNK * BLOCK // PIECE)]
    square = (BLOCK, BLOCK)
    unit = (
        lax.broadcasted_iota(jnp.int32, square, 0) == lax.broadcasted_iota(jnp.int32, square, 1)
    ).astype(jnp.bfloat16)

    def block_of(step):
        return listed[2 * blocks + 1, step]

    def arrival(j):
        return pltpu.make_async_copy(pieces[j], pairs.at[pl.ds(j * span, span)], loading[1].at[j])

    def arrive(b, i):
        ready = loading[0]
        last = lax.div(listed[b, i * CHUNK + CHUNK - 1], span) + 1
        needed = jnp.where(i >= listed[2 * blocks, b] - 1, shards, last)
        for j in range(shards):

            @pl.when((j >= ready[0]) & (j < needed))
            def _():
                arrival(j).wait()
                if j + WAVE < shards:
                    arrival(j + WAVE).start()

        ready[0] = jnp.maximum(ready[0], needed)

    def rows_of(b):
        return pl.ds(pl.multiple_of(b * BLOCK, BLOCK), BLOCK)

    def columns(g):
        return slice(g * width, (g + 1) * width)

    def keys_of(b, i):
        return jnp.concatenate([pairs[listed[b, i * CHUNK + c], :, :HEAD_DIM] for c in range(CHUNK)], axis=0)

    def values_of(b, i):
        slots = [listed[blocks + b, i * CHUNK + c] for c in range(CHUNK)]
        return jnp.concatenate(
            [
                jnp.concatenate([pairs[s, :, HEAD_DIM:] for s in slots], axis=1),
                jnp.concatenate([ones[(s == count).astype(jnp.int32)] for s in slots], axis=1),
            ],
            axis=0,
        )

    def score(b, keys, g):
        first = g * GROUP_HEADS
        tile = jnp.concatenate(
            [
                queries[rows_of(b), h * HEAD_DIM : (h + 1) * HEAD_DIM]
                for h in range(first, first + GROUP_HEADS)
            ],
            axis=0,
        )
        return lax.dot_general(keys, tile, (((1,), (1,)), ((), ())), preferred_element_type=jnp.float32)

    def partial_max(piece):
        return jnp.max(piece.reshape(-1, 8, width), axis=0)

    def first_scores(b):
        keys = keys_of(b, 0)
        for g in range(2):
            raw[g][...] = score(b, keys, g)

    def reset():
        total[...] = jnp.zeros(total.shape, jnp.float32)
        peak[...] = jnp.full(peak.shape, -jnp.inf, jnp.float32)
        soft[1][...] = jnp.zeros(soft[1].shape, jnp.bfloat16)
        late_fade[...] = jnp.ones(late_fade.shape, jnp.float32)
        level[...] = jnp.max(partial_max(raw[0][...]), axis=0, keepdims=True) * scale
        peak[:, columns(0)] = level[...]
        fade[...] = jnp.zeros(fade.shape, jnp.float32)

    ones[0] = jnp.ones(ones.shape[1:], jnp.bfloat16)
    ones[1] = jnp.zeros(ones.shape[1:], jnp.bfloat16)
    if loads:
        for j in range(WAVE):
            arrival(j).start()
        loading[0][0] = 0
        pairs[count] = jnp.zeros(pairs.shape[1:], jnp.bfloat16)
        arrive(block_of(steps[0]), 0)
    first_scores(block_of(steps[0]))
    reset()

    def visit_block(step, _):
        b = block_of(step)
        end = listed[2 * blocks, b]

        def visit(i, _):
            following = jnp.minimum(i + 1, end - 1)

            if loads:

                @pl.when(step == steps[0])
                def _():
                    arrive(b, following)

            keys = keys_of(b, i)
            next_keys = keys_of(b, following)
            values = values_of(b, i)
            before = values_of(b, jnp.maximum(i - 1, 0))
            new, factor, late = level[...], fade[...], late_fade[...]
            for g in range(groups):
                ahead, upcoming, done = (g + 2) % groups, (g + 1) % groups, (g - 1) % groups
                source = keys if g + 2 < groups else next_keys
                multiplier = values if g else before
                into = columns(done)
                total[:, into] = total[:, into] * late
                tops = None
                for cut in cuts:
                    raw[ahead][cut, :] = score(b, source[cut, :], ahead)
                    soft[g % 2][cut, :] = jnp.exp2(raw[g][cut, :] * scale - new).astype(jnp.bfloat16)
                    total[:, into] += jnp.dot(
                        multiplier[:, cut], soft[(g + 1) % 2][cut, :], preferred_element_type=jnp.float32
                    )
                    most = partial_max(raw[upcoming][cut, :])
                    tops = most if tops is None else jnp.maximum(tops, most)
                at = columns(upcoming)
                old = peak[:, at]
                new = jnp.maximum(old, jnp.max(tops, axis=0, keepdims=True) * scale)
                peak[:, at] = new
                factor, late = jnp.exp2(old - new), factor
            level[...] = new
            fade[...] = factor
            late_fade[...] = late
            return 0

        lax.fori_loop(0, end, visit, 0)
        at = columns(groups - 1)
        total[:, at] = total[:, at] * late_fade[...] + jnp.dot(
            values_of(b, end - 1), soft[1][...], preferred_element_type=jnp.float32
        )
        first_scores(block_of(jnp.minimum(step + 1, steps[1] - 1)))
        for h in range(heads):
            at = slice(h * BLOCK, (h + 1) * BLOCK)
            inverse = 1.0 / total[HEAD_DIM : HEAD_DIM + 1, at]
            normed = (total[:HEAD_DIM, at] * inverse).astype(jnp.bfloat16)
            turned = lax.dot_general(
                unit, normed, (((1,), (1,)), ((), ())), preferred_element_type=jnp.float32
            )
            out[rows_of(step - steps[0]), h * HEAD_DIM : (h + 1) * HEAD_DIM] = turned.astype(jnp.bfloat16)
        reset()
        return 0

    lax.fori_loop(*steps, visit_block, 0)


def attend(queries, sources, lists, steps):
    rows, width = queries.shape
    heads = width // HEAD_DIM
    blocks = rows // BLOCK
    loads = isinstance(sources, list)
    pair_estimate = 22 * (steps[1] - steps[0]) * 2 * 2 * heads * BLOCK * BLOCK * HEAD_DIM
    vmem = pl.BlockSpec(memory_space=pltpu.VMEM)
    out_specs, out_shape = [vmem], [jax.ShapeDtypeStruct(((steps[1] - steps[0]) * BLOCK, width), jnp.bfloat16)]
    if loads:
        shards = len(sources)
        span = sources[0].shape[0] // BLOCK
        count = shards * span
        sources = [
            pltpu.with_memory_space_constraint(piece.reshape(span, BLOCK, -1), pltpu.HBM) for piece in sources
        ]
        in_specs = [pl.BlockSpec(memory_space=pl.ANY)] * shards
        loading = [pltpu.SMEM((1,), jnp.int32), pltpu.SemaphoreType.DMA((shards,))]
        out_specs.append(vmem)
        out_shape.append(jax.ShapeDtypeStruct((count + 1, BLOCK, 2 * HEAD_DIM), jnp.bfloat16))
    else:
        shards = (sources.shape[0] - 1) // blocks
        sources, in_specs, loading = [sources], [vmem], []
    return pl.pallas_call(
        functools.partial(
            attend_kernel, blocks=blocks, steps=steps, heads=heads, shards=shards, loads=loads
        ),
        in_specs=[pl.BlockSpec(memory_space=pltpu.SMEM), vmem, *in_specs],
        out_specs=out_specs,
        scratch_shapes=[
            pltpu.VMEM((2, 16, BLOCK), jnp.bfloat16),
            pltpu.VMEM((HEAD_DIM + 16, heads * BLOCK), jnp.float32),
            pltpu.VMEM((1, heads * BLOCK), jnp.float32),
        ]
        + [pltpu.VMEM((CHUNK * BLOCK, GROUP_HEADS * BLOCK), jnp.float32)] * (heads // GROUP_HEADS)
        + [pltpu.VMEM((CHUNK * BLOCK, GROUP_HEADS * BLOCK), jnp.bfloat16)] * 2
        + [pltpu.VMEM((1, GROUP_HEADS * BLOCK), jnp.float32)] * 3
        + loading,
        out_shape=out_shape,
        compiler_params=pltpu.CompilerParams(vmem_limit_bytes=32 * 1024 * 1024),
        cost_estimate=pl.CostEstimate(flops=pair_estimate * 3, bytes_accessed=6_000_000, transcendentals=0),
    )(lists, queries, *sources)


def assemble_kernel(listed, *refs):
    *parts, out, sem = refs
    width = parts[0].shape[1]
    copies = [
        pltpu.make_async_copy(
            part, out.at[:, pl.ds(pl.multiple_of(listed[2 * len(parts) + 2, r] * width, width), width)], sem.at[r]
        )
        for r, part in enumerate(parts)
    ]
    for copy in copies:
        copy.start()
    for copy in copies:
        copy.wait()


def assemble(lists, parts):
    rows, width = parts[0].shape
    return pl.pallas_call(
        assemble_kernel,
        in_specs=[pl.BlockSpec(memory_space=pltpu.SMEM)] + [pl.BlockSpec(memory_space=pltpu.VMEM)] * len(parts),
        out_specs=pl.BlockSpec(memory_space=pl.ANY),
        out_shape=jax.ShapeDtypeStruct((rows, width * len(parts)), parts[0].dtype),
        scratch_shapes=[pltpu.SemaphoreType.DMA((len(parts),))],
    )(lists, *parts)


def shift(array, axis, step):
    size = lax.axis_size(axis)
    return lax.ppermute(array, axis, [(i, (i + step) % size) for i in range(size)])


def gather_shards(own):
    across = shift(own, "y_lo", 1)
    up, down = shift(own, "x", -1), shift(own, "x", 1)
    here = [own, up, shift(down, "x", 1), down]
    there = [across, shift(across, "x", -1), None, shift(across, "x", 1)]
    up_too, down_too = shift(up, "core", 1), shift(down, "core", 1)
    there[1], up_too, down_too = lax.optimization_barrier((there[1], up_too, down_too))
    there[2] = shift(there[1], "x", -1)
    other = [shift(own, "core", 1), up_too, shift(here[2], "core", 1), down_too]
    return here + there + other + [shift(piece, "core", 1) for piece in there]


def local(queries, keys, values, live_keys, live_count):
    head_axes, blk_axes = ("y_hi", "z"), ("x", "y_lo", "core")
    parts = lax.axis_size(head_axes)
    tokens = queries.shape[0]
    sizes = tuple(lax.axis_size(axis) for axis in blk_axes + head_axes)
    blocks = parts * tokens // BLOCK

    def exchange(cut):
        moved = lax.all_to_all(cut, head_axes, split_axis=0, concat_axis=0, tiled=True)
        return moved.reshape(parts * tokens, -1)

    def cut(array):
        return array.reshape(tokens, parts, -1)

    own = exchange(pack(keys, values, parts))
    y_size, z_size = (lax.axis_size(axis) for axis in head_axes)
    far = [(dy, dz) for dy in range(y_size) for dz in range(z_size)]
    far.sort(key=lambda d: (d[0] + min(d[1], z_size - d[1]), d[0]), reverse=True)

    def at_distance(y, z, dy, dz):
        return (y + dy) % y_size * z_size + (z + dz) % z_size

    place = jnp.stack([lax.axis_index(axis) for axis in blk_axes + head_axes]).astype(jnp.int32)
    lists = plan(place, live_keys, live_count, blocks, sizes, live_keys.shape[0] * blocks, far)
    own, lists, query_parts = lax.optimization_barrier((own, lists, cut(queries).transpose(1, 0, 2)))
    pieces = gather_shards(own)
    query_local = exchange(query_parts)

    def send(attended, steps):
        sent = []
        for step in range(*steps):
            part = attended[(step - steps[0]) * tokens : (step - steps[0] + 1) * tokens]
            if any(far[step]):
                pairs = [
                    (k, at_distance(k // z_size, k % z_size, *far[step])) for k in range(y_size * z_size)
                ]
                part = lax.ppermute(part, head_axes, pairs)
            sent.append(part)
        return sent

    early, late = (0, FIRST_STEPS), (FIRST_STEPS, parts)
    attended, gathered = attend(query_local, pieces, lists, early)
    received = send(attended, early)
    (attended,) = attend(query_local, gathered, lists, late)
    attended, received = lax.optimization_barrier((attended, received))
    received += send(attended, late)
    return assemble(lists, received)


def solution(mesh):
    fine = Mesh(mesh.devices.reshape(4, 2, 2, 2, 4), ("x", "y_lo", "core", "y_hi", "z"))
    rows = P(("x", "y_lo", "core", "y_hi", "z"), None)
    return jax.shard_map(
        local,
        mesh=fine,
        in_specs=(rows, rows, rows, P(), P()),
        out_specs=rows,
        check_vma=False,
    )
```

```python
import functools

import jax
import jax.numpy as jnp
from jax import lax
from jax.experimental import pallas as pl
from jax.experimental.pallas import tpu as pltpu
from jax.sharding import Mesh
from jax.sharding import PartitionSpec as P

HEADS = 64
KV_HEADS = 8
HEAD_DIM = 128
BLOCK = 128
LOG2E = 1.4426950408889634
CHUNK = 4
GROUP_HEADS = 2
PIECE = 512
WAVE = 8
FIRST_STEPS = 5


def pack_kernel(keys, values, out):
    for h in range(out.shape[0]):
        at = slice(h * HEAD_DIM, (h + 1) * HEAD_DIM)
        out[h, :, :HEAD_DIM] = keys[:, at]
        out[h, :, HEAD_DIM:] = values[:, at].T


def pack(keys, values, parts):
    tokens = keys.shape[0]
    vmem = pl.BlockSpec(memory_space=pltpu.VMEM)
    return pl.pallas_call(
        pack_kernel,
        in_specs=[vmem, vmem],
        out_specs=vmem,
        out_shape=jax.ShapeDtypeStruct((parts, tokens, 2 * HEAD_DIM), keys.dtype),
    )(keys, values)


def plan_kernel(place_ref, codes_ref, counts_ref, list_ref, fill_ref, *, blocks, sizes, zero, far):
    x_size, y_lo_size, core_size = sizes[:3]
    x, y, core = place_ref[0], place_ref[1], place_ref[2]
    shard = (x * y_lo_size + y) * core_size + core
    for a in range(blocks):
        list_ref[a, 0] = a
        list_ref[blocks + a, 0] = a
        fill_ref[a] = 1

    y_hi, z = place_ref[3], place_ref[4]
    y_size, z_size = sizes[3:]
    for step, (dy, dz) in enumerate(far):
        for row, sign in ((1, 1), (2, -1)):
            to_y = lax.rem(y_hi + sign * dy + y_size, y_size)
            to_z = lax.rem(z + sign * dz + z_size, z_size)
            list_ref[2 * blocks + row, step] = to_y * z_size + to_z

    def visit_shard(slot, _):
        from_x = lax.rem(x + lax.rem(slot, x_size), x_size)
        from_y = lax.rem(y + lax.rem(lax.div(slot, x_size), y_lo_size), y_lo_size)
        from_core = lax.rem(core + lax.div(slot, x_size * y_lo_size), core_size)
        j = (from_x * y_lo_size + from_y) * core_size + from_core

        def visit_entry(c, _):
            code = codes_ref[shard, j, c]
            a = lax.div(code, blocks)
            block = slot * blocks + lax.rem(code, blocks)
            at = fill_ref[a]
            list_ref[a, at] = block
            list_ref[blocks + a, at] = block
            fill_ref[a] = at + 1
            return 0

        return lax.fori_loop(0, counts_ref[shard, j], visit_entry, 0)

    lax.fori_loop(0, x_size * y_lo_size * core_size, visit_shard, 0)
    for a in range(blocks):
        filled = fill_ref[a]
        chunks = lax.div(filled + CHUNK - 1, CHUNK)
        list_ref[2 * blocks, a] = chunks

        def pad(at, _):
            list_ref[a, at] = a
            list_ref[blocks + a, at] = zero
            return 0

        lax.fori_loop(filled, chunks * CHUNK, pad, 0)


def plan(place, live_keys, live_count, blocks, sizes, zero, far):
    shards = live_keys.shape[0]
    width = -(-(shards * blocks + 1) // CHUNK) * CHUNK
    smem = pl.BlockSpec(memory_space=pltpu.SMEM)
    return pl.pallas_call(
        functools.partial(plan_kernel, blocks=blocks, sizes=sizes, zero=zero, far=far),
        in_specs=[smem] * 3,
        out_specs=smem,
        out_shape=jax.ShapeDtypeStruct((2 * blocks + 3, width), jnp.int32),
        scratch_shapes=[pltpu.SMEM((blocks,), jnp.int32)],
        cost_estimate=pl.CostEstimate(flops=0, bytes_accessed=20_000_000, transcendentals=0),
    )(place, live_keys, live_count)


def attend_kernel(listed, queries, *refs, blocks, steps, heads, shards, loads):
    if loads:
        pieces, (out, pairs, *rest) = refs[:shards], refs[shards:]
    else:
        pairs, out, *rest = refs
    ones, total, peak, *rest = rest
    groups = heads // GROUP_HEADS
    raw, soft, (level, fade, late_fade, *loading) = rest[:groups], rest[groups : groups + 2], rest[groups + 2 :]
    count = pairs.shape[0] - 1
    span = count // shards
    width = GROUP_HEADS * BLOCK
    scale = HEAD_DIM**-0.5 * LOG2E
    cuts = [slice(j * PIECE, (j + 1) * PIECE) for j in range(CHUNK * BLOCK // PIECE)]
    square = (BLOCK, BLOCK)
    unit = (
        lax.broadcasted_iota(jnp.int32, square, 0) == lax.broadcasted_iota(jnp.int32, square, 1)
    ).astype(jnp.bfloat16)

    def block_of(step):
        return listed[2 * blocks + 1, step]

    def arrival(j):
        return pltpu.make_async_copy(pieces[j], pairs.at[pl.ds(j * span, span)], loading[1].at[j])

    def arrive(b, i):
        ready = loading[0]
        last = lax.div(listed[b, i * CHUNK + CHUNK - 1], span) + 1
        needed = jnp.where(i >= listed[2 * blocks, b] - 1, shards, last)
        for j in range(shards):

            @pl.when((j >= ready[0]) & (j < needed))
            def _():
                arrival(j).wait()
                if j + WAVE < shards:
                    arrival(j + WAVE).start()

        ready[0] = jnp.maximum(ready[0], needed)

    def rows_of(b):
        return pl.ds(pl.multiple_of(b * BLOCK, BLOCK), BLOCK)

    def columns(g):
        return slice(g * width, (g + 1) * width)

    def keys_of(b, i):
        return jnp.concatenate([pairs[listed[b, i * CHUNK + c], :, :HEAD_DIM] for c in range(CHUNK)], axis=0)

    def values_of(b, i):
        slots = [listed[blocks + b, i * CHUNK + c] for c in range(CHUNK)]
        return jnp.concatenate(
            [
                jnp.concatenate([pairs[s, :, HEAD_DIM:] for s in slots], axis=1),
                jnp.concatenate([ones[(s == count).astype(jnp.int32)] for s in slots], axis=1),
            ],
            axis=0,
        )

    def score(b, keys, g):
        first = g * GROUP_HEADS
        tile = jnp.concatenate(
            [
                queries[rows_of(b), h * HEAD_DIM : (h + 1) * HEAD_DIM]
                for h in range(first, first + GROUP_HEADS)
            ],
            axis=0,
        )
        return lax.dot_general(keys, tile, (((1,), (1,)), ((), ())), preferred_element_type=jnp.float32)

    def partial_max(piece):
        return jnp.max(piece.reshape(-1, 8, width), axis=0)

    def first_scores(b):
        keys = keys_of(b, 0)
        for g in range(2):
            raw[g][...] = score(b, keys, g)

    def reset():
        total[...] = jnp.zeros(total.shape, jnp.float32)
        peak[...] = jnp.full(peak.shape, -jnp.inf, jnp.float32)
        soft[1][...] = jnp.zeros(soft[1].shape, jnp.bfloat16)
        late_fade[...] = jnp.ones(late_fade.shape, jnp.float32)
        level[...] = jnp.max(partial_max(raw[0][...]), axis=0, keepdims=True) * scale
        peak[:, columns(0)] = level[...]
        fade[...] = jnp.zeros(fade.shape, jnp.float32)

    ones[0] = jnp.ones(ones.shape[1:], jnp.bfloat16)
    ones[1] = jnp.zeros(ones.shape[1:], jnp.bfloat16)
    if loads:
        for j in range(WAVE):
            arrival(j).start()
        loading[0][0] = 0
        pairs[count] = jnp.zeros(pairs.shape[1:], jnp.bfloat16)
        arrive(block_of(steps[0]), 0)
    first_scores(block_of(steps[0]))
    reset()

    def visit_block(step, _):
        b = block_of(step)
        end = listed[2 * blocks, b]

        def visit(i, _):
            following = jnp.minimum(i + 1, end - 1)

            if loads:

                @pl.when(step == steps[0])
                def _():
                    arrive(b, following)

            keys = keys_of(b, i)
            next_keys = keys_of(b, following)
            values = values_of(b, i)
            before = values_of(b, jnp.maximum(i - 1, 0))
            new, factor, late = level[...], fade[...], late_fade[...]
            for g in range(groups):
                ahead, upcoming, done = (g + 2) % groups, (g + 1) % groups, (g - 1) % groups
                source = keys if g + 2 < groups else next_keys
                multiplier = values if g else before
                into = columns(done)
                total[:, into] = total[:, into] * late
                tops = None
                for cut in cuts:
                    raw[ahead][cut, :] = score(b, source[cut, :], ahead)
                    soft[g % 2][cut, :] = jnp.exp2(raw[g][cut, :] * scale - new).astype(jnp.bfloat16)
                    total[:, into] += jnp.dot(
                        multiplier[:, cut], soft[(g + 1) % 2][cut, :], preferred_element_type=jnp.float32
                    )
                    most = partial_max(raw[upcoming][cut, :])
                    tops = most if tops is None else jnp.maximum(tops, most)
                at = columns(upcoming)
                old = peak[:, at]
                new = jnp.maximum(old, jnp.max(tops, axis=0, keepdims=True) * scale)
                peak[:, at] = new
                factor, late = jnp.exp2(old - new), factor
            level[...] = new
            fade[...] = factor
            late_fade[...] = late
            return 0

        lax.fori_loop(0, end, visit, 0)
        at = columns(groups - 1)
        total[:, at] = total[:, at] * late_fade[...] + jnp.dot(
            values_of(b, end - 1), soft[1][...], preferred_element_type=jnp.float32
        )
        first_scores(block_of(jnp.minimum(step + 1, steps[1] - 1)))
        for h in range(heads):
            at = slice(h * BLOCK, (h + 1) * BLOCK)
            inverse = 1.0 / total[HEAD_DIM : HEAD_DIM + 1, at]
            normed = (total[:HEAD_DIM, at] * inverse).astype(jnp.bfloat16)
            turned = lax.dot_general(
                unit, normed, (((1,), (1,)), ((), ())), preferred_element_type=jnp.float32
            )
            out[rows_of(step - steps[0]), h * HEAD_DIM : (h + 1) * HEAD_DIM] = turned.astype(jnp.bfloat16)
        reset()
        return 0

    lax.fori_loop(*steps, visit_block, 0)


def attend(queries, sources, lists, steps):
    rows, width = queries.shape
    heads = width // HEAD_DIM
    blocks = rows // BLOCK
    loads = isinstance(sources, list)
    pair_estimate = 22 * (steps[1] - steps[0]) * 2 * 2 * heads * BLOCK * BLOCK * HEAD_DIM
    vmem = pl.BlockSpec(memory_space=pltpu.VMEM)
    out_specs, out_shape = [vmem], [jax.ShapeDtypeStruct(((steps[1] - steps[0]) * BLOCK, width), jnp.bfloat16)]
    if loads:
        shards = len(sources)
        span = sources[0].shape[0] // BLOCK
        count = shards * span
        sources = [
            pltpu.with_memory_space_constraint(piece.reshape(span, BLOCK, -1), pltpu.HBM) for piece in sources
        ]
        in_specs = [pl.BlockSpec(memory_space=pl.ANY)] * shards
        loading = [pltpu.SMEM((1,), jnp.int32), pltpu.SemaphoreType.DMA((shards,))]
        out_specs.append(vmem)
        out_shape.append(jax.ShapeDtypeStruct((count + 1, BLOCK, 2 * HEAD_DIM), jnp.bfloat16))
    else:
        shards = (sources.shape[0] - 1) // blocks
        sources, in_specs, loading = [sources], [vmem], []
    return pl.pallas_call(
        functools.partial(
            attend_kernel, blocks=blocks, steps=steps, heads=heads, shards=shards, loads=loads
        ),
        in_specs=[pl.BlockSpec(memory_space=pltpu.SMEM), vmem, *in_specs],
        out_specs=out_specs,
        scratch_shapes=[
            pltpu.VMEM((2, 16, BLOCK), jnp.bfloat16),
            pltpu.VMEM((HEAD_DIM + 16, heads * BLOCK), jnp.float32),
            pltpu.VMEM((1, heads * BLOCK), jnp.float32),
        ]
        + [pltpu.VMEM((CHUNK * BLOCK, GROUP_HEADS * BLOCK), jnp.float32)] * (heads // GROUP_HEADS)
        + [pltpu.VMEM((CHUNK * BLOCK, GROUP_HEADS * BLOCK), jnp.bfloat16)] * 2
        + [pltpu.VMEM((1, GROUP_HEADS * BLOCK), jnp.float32)] * 3
        + loading,
        out_shape=out_shape,
        compiler_params=pltpu.CompilerParams(vmem_limit_bytes=32 * 1024 * 1024),
        cost_estimate=pl.CostEstimate(flops=pair_estimate * 3, bytes_accessed=6_000_000, transcendentals=0),
    )(lists, pltpu.with_memory_space_constraint(queries, pltpu.VMEM), *sources)


def assemble_kernel(listed, *refs):
    *parts, late, out, sem = refs
    tokens, width = out.shape[0], late.shape[1]
    count = out.shape[1] // width
    copies = []
    for r in range(count):
        at = pl.ds(pl.multiple_of(listed[2 * count + 2, r] * width, width), width)
        source = parts[r] if r < len(parts) else late.at[pl.ds(late.shape[0] - tokens, tokens)]
        copies.append(pltpu.make_async_copy(source, out.at[:, at], sem.at[r]))
    for copy in copies:
        copy.start()
    for copy in copies:
        copy.wait()


def assemble(lists, parts, late):
    rows, width = parts[0].shape
    count = len(parts) + 1
    spaces = [pltpu.HBM] * FIRST_STEPS + [pltpu.VMEM] * (count - FIRST_STEPS)
    parts = [
        pltpu.with_memory_space_constraint(part, space)
        for part, space in zip([*parts, late], spaces, strict=True)
    ]
    return pl.pallas_call(
        assemble_kernel,
        in_specs=[pl.BlockSpec(memory_space=pltpu.SMEM)] + [pl.BlockSpec(memory_space=pl.ANY)] * count,
        out_specs=pl.BlockSpec(memory_space=pl.ANY),
        out_shape=jax.ShapeDtypeStruct((rows, width * count), late.dtype),
        scratch_shapes=[pltpu.SemaphoreType.DMA((count,))],
    )(lists, *parts)


def shift(array, axis, step):
    size = lax.axis_size(axis)
    return lax.ppermute(array, axis, [(i, (i + step) % size) for i in range(size)])


def gather_shards(own):
    across = shift(own, "y_lo", 1)
    up, down = shift(own, "x", -1), shift(own, "x", 1)
    here = [own, up, shift(down, "x", 1), down]
    there = [across, shift(across, "x", -1), None, shift(across, "x", 1)]
    up_too, down_too = shift(up, "core", 1), shift(down, "core", 1)
    there[1], up_too, down_too = lax.optimization_barrier((there[1], up_too, down_too))
    there[2] = shift(there[1], "x", -1)
    other = [shift(own, "core", 1), up_too, shift(here[2], "core", 1), down_too]
    return here + there + other + [shift(piece, "core", 1) for piece in there]


def local(queries, keys, values, live_keys, live_count):
    head_axes, blk_axes = ("y_hi", "z"), ("x", "y_lo", "core")
    parts = lax.axis_size(head_axes)
    tokens = queries.shape[0]
    sizes = tuple(lax.axis_size(axis) for axis in blk_axes + head_axes)
    blocks = parts * tokens // BLOCK

    def exchange(cut):
        moved = lax.all_to_all(cut, head_axes, split_axis=0, concat_axis=0, tiled=True)
        return moved.reshape(parts * tokens, -1)

    def cut(array):
        return array.reshape(tokens, parts, -1)

    own = exchange(pack(keys, values, parts))
    y_size, z_size = (lax.axis_size(axis) for axis in head_axes)
    far = [(dy, dz) for dy in range(y_size) for dz in range(z_size)]
    far.sort(key=lambda d: (d[0] + min(d[1], z_size - d[1]), d[0]), reverse=True)

    def at_distance(y, z, dy, dz):
        return (y + dy) % y_size * z_size + (z + dz) % z_size

    place = jnp.stack([lax.axis_index(axis) for axis in blk_axes + head_axes]).astype(jnp.int32)
    lists = plan(place, live_keys, live_count, blocks, sizes, live_keys.shape[0] * blocks, far)
    own, lists, query_parts = lax.optimization_barrier((own, lists, cut(queries).transpose(1, 0, 2)))
    pieces = gather_shards(own)
    query_local = exchange(query_parts)

    def send(attended, steps):
        sent = []
        for step in range(*steps):
            part = attended[(step - steps[0]) * tokens : (step - steps[0] + 1) * tokens]
            pairs = [(k, at_distance(k // z_size, k % z_size, *far[step])) for k in range(y_size * z_size)]
            sent.append(lax.ppermute(part, head_axes, pairs))
        return sent

    early, late = (0, FIRST_STEPS), (FIRST_STEPS, parts)
    attended, gathered = attend(query_local, pieces, lists, early)
    received = send(attended, early)
    (attended,) = attend(query_local, gathered, lists, late)
    attended, received = lax.optimization_barrier((attended, received))
    received += send(attended, (FIRST_STEPS, parts - 1))
    return assemble(lists, received, attended)


def solution(mesh):
    fine = Mesh(mesh.devices.reshape(4, 2, 2, 2, 4), ("x", "y_lo", "core", "y_hi", "z"))
    rows = P(("x", "y_lo", "core", "y_hi", "z"), None)
    return jax.shard_map(
        local,
        mesh=fine,
        in_specs=(rows, rows, rows, P(), P()),
        out_specs=rows,
        check_vma=False,
    )
```

```python
import functools

import jax
import jax.numpy as jnp
from jax import lax
from jax.experimental import pallas as pl
from jax.experimental.pallas import tpu as pltpu
from jax.sharding import Mesh
from jax.sharding import PartitionSpec as P

HEADS = 64
KV_HEADS = 8
HEAD_DIM = 128
BLOCK = 128
LOG2E = 1.4426950408889634
CHUNK = 4
GROUP_HEADS = 2
PIECE = 512
WAVE = 8
FIRST_STEPS = 5


def pack_kernel(keys, values, out):
    for h in range(out.shape[0]):
        at = slice(h * HEAD_DIM, (h + 1) * HEAD_DIM)
        out[h, :, :HEAD_DIM] = keys[:, at]
        out[h, :, HEAD_DIM:] = values[:, at].T


def pack(keys, values, parts):
    tokens = keys.shape[0]
    vmem = pl.BlockSpec(memory_space=pltpu.VMEM)
    return pl.pallas_call(
        pack_kernel,
        in_specs=[vmem, vmem],
        out_specs=vmem,
        out_shape=jax.ShapeDtypeStruct((parts, tokens, 2 * HEAD_DIM), keys.dtype),
    )(keys, values)


def plan_kernel(place_ref, codes_ref, counts_ref, list_ref, fill_ref, *, blocks, sizes, zero, far):
    x_size, y_lo_size, core_size = sizes[:3]
    x, y, core = place_ref[0], place_ref[1], place_ref[2]
    shard = (x * y_lo_size + y) * core_size + core
    for a in range(blocks):
        list_ref[a, 0] = a
        list_ref[blocks + a, 0] = a
        fill_ref[a] = 1

    y_hi, z = place_ref[3], place_ref[4]
    y_size, z_size = sizes[3:]
    for step, (dy, dz) in enumerate(far):
        for row, sign in ((1, 1), (2, -1)):
            to_y = lax.rem(y_hi + sign * dy + y_size, y_size)
            to_z = lax.rem(z + sign * dz + z_size, z_size)
            list_ref[2 * blocks + row, step] = to_y * z_size + to_z

    def visit_shard(slot, _):
        from_x = lax.rem(x + lax.rem(slot, x_size), x_size)
        from_y = lax.rem(y + lax.rem(lax.div(slot, x_size), y_lo_size), y_lo_size)
        from_core = lax.rem(core + lax.div(slot, x_size * y_lo_size), core_size)
        j = (from_x * y_lo_size + from_y) * core_size + from_core

        def visit_entry(c, _):
            code = codes_ref[shard, j, c]
            a = lax.div(code, blocks)
            block = slot * blocks + lax.rem(code, blocks)
            at = fill_ref[a]
            list_ref[a, at] = block
            list_ref[blocks + a, at] = block
            fill_ref[a] = at + 1
            return 0

        return lax.fori_loop(0, counts_ref[shard, j], visit_entry, 0)

    lax.fori_loop(0, x_size * y_lo_size * core_size, visit_shard, 0)
    for a in range(blocks):
        filled = fill_ref[a]
        chunks = lax.div(filled + CHUNK - 1, CHUNK)
        list_ref[2 * blocks, a] = chunks

        def pad(at, _):
            list_ref[a, at] = a
            list_ref[blocks + a, at] = zero
            return 0

        lax.fori_loop(filled, chunks * CHUNK, pad, 0)


def plan(place, live_keys, live_count, blocks, sizes, zero, far):
    shards = live_keys.shape[0]
    width = -(-(shards * blocks + 1) // CHUNK) * CHUNK
    smem = pl.BlockSpec(memory_space=pltpu.SMEM)
    return pl.pallas_call(
        functools.partial(plan_kernel, blocks=blocks, sizes=sizes, zero=zero, far=far),
        in_specs=[smem] * 3,
        out_specs=smem,
        out_shape=jax.ShapeDtypeStruct((2 * blocks + 3, width), jnp.int32),
        scratch_shapes=[pltpu.SMEM((blocks,), jnp.int32)],
        cost_estimate=pl.CostEstimate(flops=0, bytes_accessed=20_000_000, transcendentals=0),
    )(place, live_keys, live_count)


def attend_kernel(listed, queries, *refs, blocks, steps, heads, shards, loads):
    if loads:
        pieces, (out, pairs, *rest) = refs[:shards], refs[shards:]
    else:
        pairs, out, *rest = refs
    ones, total, peak, *rest = rest
    groups = heads // GROUP_HEADS
    raw, soft, (level, fade, late_fade, *loading) = rest[:groups], rest[groups : groups + 2], rest[groups + 2 :]
    count = pairs.shape[0] - 1
    span = count // shards
    width = GROUP_HEADS * BLOCK
    scale = HEAD_DIM**-0.5 * LOG2E
    cuts = [slice(j * PIECE, (j + 1) * PIECE) for j in range(CHUNK * BLOCK // PIECE)]
    square = (BLOCK, BLOCK)
    unit = (
        lax.broadcasted_iota(jnp.int32, square, 0) == lax.broadcasted_iota(jnp.int32, square, 1)
    ).astype(jnp.bfloat16)

    def block_of(step):
        return listed[2 * blocks + 1, step]

    def arrival(j):
        return pltpu.make_async_copy(pieces[j], pairs.at[pl.ds(j * span, span)], loading[1].at[j])

    def arrive(b, i):
        ready = loading[0]
        last = lax.div(listed[b, i * CHUNK + CHUNK - 1], span) + 1
        needed = jnp.where(i >= listed[2 * blocks, b] - 1, shards, last)
        for j in range(shards):

            @pl.when((j >= ready[0]) & (j < needed))
            def _():
                arrival(j).wait()
                if j + WAVE < shards:
                    arrival(j + WAVE).start()

        ready[0] = jnp.maximum(ready[0], needed)

    def rows_of(b):
        return pl.ds(pl.multiple_of(b * BLOCK, BLOCK), BLOCK)

    def columns(g):
        return slice(g * width, (g + 1) * width)

    def keys_of(b, i):
        return jnp.concatenate([pairs[listed[b, i * CHUNK + c], :, :HEAD_DIM] for c in range(CHUNK)], axis=0)

    def values_of(b, i):
        slots = [listed[blocks + b, i * CHUNK + c] for c in range(CHUNK)]
        return jnp.concatenate(
            [
                jnp.concatenate([pairs[s, :, HEAD_DIM:] for s in slots], axis=1),
                jnp.concatenate([ones[(s == count).astype(jnp.int32)] for s in slots], axis=1),
            ],
            axis=0,
        )

    def score(b, keys, g):
        first = g * GROUP_HEADS
        tile = jnp.concatenate(
            [
                queries[rows_of(b), h * HEAD_DIM : (h + 1) * HEAD_DIM]
                for h in range(first, first + GROUP_HEADS)
            ],
            axis=0,
        )
        return lax.dot_general(keys, tile, (((1,), (1,)), ((), ())), preferred_element_type=jnp.float32)

    def partial_max(piece):
        return jnp.max(piece.reshape(-1, 8, width), axis=0)

    def first_scores(b):
        keys = keys_of(b, 0)
        for g in range(2):
            raw[g][...] = score(b, keys, g)

    def reset():
        total[...] = jnp.zeros(total.shape, jnp.float32)
        peak[...] = jnp.full(peak.shape, -jnp.inf, jnp.float32)
        soft[1][...] = jnp.zeros(soft[1].shape, jnp.bfloat16)
        late_fade[...] = jnp.ones(late_fade.shape, jnp.float32)
        level[...] = jnp.max(partial_max(raw[0][...]), axis=0, keepdims=True) * scale
        peak[:, columns(0)] = level[...]
        fade[...] = jnp.zeros(fade.shape, jnp.float32)

    ones[0] = jnp.ones(ones.shape[1:], jnp.bfloat16)
    ones[1] = jnp.zeros(ones.shape[1:], jnp.bfloat16)
    if loads:
        for j in range(WAVE):
            arrival(j).start()
        loading[0][0] = 0
        pairs[count] = jnp.zeros(pairs.shape[1:], jnp.bfloat16)
        arrive(block_of(steps[0]), 0)
    first_scores(block_of(steps[0]))
    reset()

    def visit_block(step, _):
        b = block_of(step)
        end = listed[2 * blocks, b]

        def visit(i, _):
            following = jnp.minimum(i + 1, end - 1)

            if loads:

                @pl.when(step == steps[0])
                def _():
                    arrive(b, following)

            keys = keys_of(b, i)
            next_keys = keys_of(b, following)
            values = values_of(b, i)
            before = values_of(b, jnp.maximum(i - 1, 0))
            new, factor, late = level[...], fade[...], late_fade[...]
            for g in range(groups):
                ahead, upcoming, done = (g + 2) % groups, (g + 1) % groups, (g - 1) % groups
                source = keys if g + 2 < groups else next_keys
                multiplier = values if g else before
                into = columns(done)
                total[:, into] = total[:, into] * late
                tops = None
                for cut in cuts:
                    raw[ahead][cut, :] = score(b, source[cut, :], ahead)
                    soft[g % 2][cut, :] = jnp.exp2(raw[g][cut, :] * scale - new).astype(jnp.bfloat16)
                    total[:, into] += jnp.dot(
                        multiplier[:, cut], soft[(g + 1) % 2][cut, :], preferred_element_type=jnp.float32
                    )
                    most = partial_max(raw[upcoming][cut, :])
                    tops = most if tops is None else jnp.maximum(tops, most)
                at = columns(upcoming)
                old = peak[:, at]
                new = jnp.maximum(old, jnp.max(tops, axis=0, keepdims=True) * scale)
                peak[:, at] = new
                factor, late = jnp.exp2(old - new), factor
            level[...] = new
            fade[...] = factor
            late_fade[...] = late
            return 0

        lax.fori_loop(0, end, visit, 0)
        at = columns(groups - 1)
        total[:, at] = total[:, at] * late_fade[...] + jnp.dot(
            values_of(b, end - 1), soft[1][...], preferred_element_type=jnp.float32
        )
        first_scores(block_of(jnp.minimum(step + 1, steps[1] - 1)))
        for h in range(heads):
            at = slice(h * BLOCK, (h + 1) * BLOCK)
            inverse = 1.0 / total[HEAD_DIM : HEAD_DIM + 1, at]
            normed = (total[:HEAD_DIM, at] * inverse).astype(jnp.bfloat16)
            turned = lax.dot_general(
                unit, normed, (((1,), (1,)), ((), ())), preferred_element_type=jnp.float32
            )
            out[rows_of(step - steps[0]), h * HEAD_DIM : (h + 1) * HEAD_DIM] = turned.astype(jnp.bfloat16)
        reset()
        return 0

    lax.fori_loop(*steps, visit_block, 0)


def attend(queries, sources, lists, steps):
    rows, width = queries.shape
    heads = width // HEAD_DIM
    blocks = rows // BLOCK
    loads = isinstance(sources, list)
    pair_estimate = 22 * (steps[1] - steps[0]) * 2 * 2 * heads * BLOCK * BLOCK * HEAD_DIM
    vmem = pl.BlockSpec(memory_space=pltpu.VMEM)
    out_specs, out_shape = [vmem], [jax.ShapeDtypeStruct(((steps[1] - steps[0]) * BLOCK, width), jnp.bfloat16)]
    if loads:
        shards = len(sources)
        span = sources[0].shape[0] // BLOCK
        count = shards * span
        sources = [
            pltpu.with_memory_space_constraint(piece.reshape(span, BLOCK, -1), pltpu.HBM) for piece in sources
        ]
        in_specs = [pl.BlockSpec(memory_space=pl.ANY)] * shards
        loading = [pltpu.SMEM((1,), jnp.int32), pltpu.SemaphoreType.DMA((shards,))]
        out_specs.append(vmem)
        out_shape.append(jax.ShapeDtypeStruct((count + 1, BLOCK, 2 * HEAD_DIM), jnp.bfloat16))
    else:
        shards = (sources.shape[0] - 1) // blocks
        sources, in_specs, loading = [sources], [vmem], []
    return pl.pallas_call(
        functools.partial(
            attend_kernel, blocks=blocks, steps=steps, heads=heads, shards=shards, loads=loads
        ),
        in_specs=[pl.BlockSpec(memory_space=pltpu.SMEM), vmem, *in_specs],
        out_specs=out_specs,
        scratch_shapes=[
            pltpu.VMEM((2, 16, BLOCK), jnp.bfloat16),
            pltpu.VMEM((HEAD_DIM + 16, heads * BLOCK), jnp.float32),
            pltpu.VMEM((1, heads * BLOCK), jnp.float32),
        ]
        + [pltpu.VMEM((CHUNK * BLOCK, GROUP_HEADS * BLOCK), jnp.float32)] * (heads // GROUP_HEADS)
        + [pltpu.VMEM((CHUNK * BLOCK, GROUP_HEADS * BLOCK), jnp.bfloat16)] * 2
        + [pltpu.VMEM((1, GROUP_HEADS * BLOCK), jnp.float32)] * 3
        + loading,
        out_shape=out_shape,
        compiler_params=pltpu.CompilerParams(vmem_limit_bytes=32 * 1024 * 1024),
        cost_estimate=pl.CostEstimate(flops=pair_estimate * 3, bytes_accessed=6_000_000, transcendentals=0),
    )(lists, pltpu.with_memory_space_constraint(queries, pltpu.VMEM), *sources)


def assemble_kernel(listed, *refs):
    *parts, late, out, sem = refs
    tokens, width = out.shape[0], late.shape[1]
    count = out.shape[1] // width
    copies = []
    for r in range(count):
        at = pl.ds(pl.multiple_of(listed[2 * count + 2, r] * width, width), width)
        source = parts[r] if r < len(parts) else late.at[pl.ds(late.shape[0] - tokens, tokens)]
        copies.append(pltpu.make_async_copy(source, out.at[:, at], sem.at[r]))
    for copy in copies:
        copy.start()
    for copy in copies:
        copy.wait()


def assemble(lists, parts, late):
    rows, width = parts[0].shape
    count = len(parts) + 1
    parts = [*parts[:FIRST_STEPS]] + [
        pltpu.with_memory_space_constraint(part, pltpu.VMEM) for part in [*parts[FIRST_STEPS:], late]
    ]
    return pl.pallas_call(
        assemble_kernel,
        in_specs=[pl.BlockSpec(memory_space=pltpu.SMEM)]
        + [pl.BlockSpec(memory_space=pltpu.VMEM)] * FIRST_STEPS
        + [pl.BlockSpec(memory_space=pl.ANY)] * (count - FIRST_STEPS),
        out_specs=pl.BlockSpec(memory_space=pl.ANY),
        out_shape=jax.ShapeDtypeStruct((rows, width * count), late.dtype),
        scratch_shapes=[pltpu.SemaphoreType.DMA((count,))],
    )(lists, *parts)


def shift(array, axis, step):
    size = lax.axis_size(axis)
    return lax.ppermute(array, axis, [(i, (i + step) % size) for i in range(size)])


def gather_shards(own):
    across = shift(own, "y_lo", 1)
    up, down = shift(own, "x", -1), shift(own, "x", 1)
    here = [own, up, shift(down, "x", 1), down]
    there = [across, shift(across, "x", -1), None, shift(across, "x", 1)]
    up_too, down_too = shift(up, "core", 1), shift(down, "core", 1)
    there[1], up_too, down_too = lax.optimization_barrier((there[1], up_too, down_too))
    there[2] = shift(there[1], "x", -1)
    other = [shift(own, "core", 1), up_too, shift(here[2], "core", 1), down_too]
    return here + there + other + [shift(piece, "core", 1) for piece in there]


def local(queries, keys, values, live_keys, live_count):
    head_axes, blk_axes = ("y_hi", "z"), ("x", "y_lo", "core")
    parts = lax.axis_size(head_axes)
    tokens = queries.shape[0]
    sizes = tuple(lax.axis_size(axis) for axis in blk_axes + head_axes)
    blocks = parts * tokens // BLOCK

    def exchange(cut):
        moved = lax.all_to_all(cut, head_axes, split_axis=0, concat_axis=0, tiled=True)
        return moved.reshape(parts * tokens, -1)

    def cut(array):
        return array.reshape(tokens, parts, -1)

    own = exchange(pack(keys, values, parts))
    y_size, z_size = (lax.axis_size(axis) for axis in head_axes)
    far = [(dy, dz) for dy in range(y_size) for dz in range(z_size)]
    far.sort(key=lambda d: (d[0] + min(d[1], z_size - d[1]), d[0]), reverse=True)

    def at_distance(y, z, dy, dz):
        return (y + dy) % y_size * z_size + (z + dz) % z_size

    place = jnp.stack([lax.axis_index(axis) for axis in blk_axes + head_axes]).astype(jnp.int32)
    lists = plan(place, live_keys, live_count, blocks, sizes, live_keys.shape[0] * blocks, far)
    own, lists, query_parts = lax.optimization_barrier((own, lists, cut(queries).transpose(1, 0, 2)))
    pieces = gather_shards(own)
    query_local = exchange(query_parts)

    def send(attended, steps):
        sent = []
        for step in range(*steps):
            part = attended[(step - steps[0]) * tokens : (step - steps[0] + 1) * tokens]
            pairs = [(k, at_distance(k // z_size, k % z_size, *far[step])) for k in range(y_size * z_size)]
            sent.append(lax.ppermute(part, head_axes, pairs))
        return sent

    early, late = (0, FIRST_STEPS), (FIRST_STEPS, parts)
    attended, gathered = attend(query_local, pieces, lists, early)
    received = send(attended, early)
    (attended,) = attend(query_local, gathered, lists, late)
    attended, received = lax.optimization_barrier((attended, received))
    received += send(attended, (FIRST_STEPS, parts - 1))
    return assemble(lists, received, attended)


def solution(mesh):
    fine = Mesh(mesh.devices.reshape(4, 2, 2, 2, 4), ("x", "y_lo", "core", "y_hi", "z"))
    rows = P(("x", "y_lo", "core", "y_hi", "z"), None)
    return jax.shard_map(
        local,
        mesh=fine,
        in_specs=(rows, rows, rows, P(), P()),
        out_specs=rows,
        check_vma=False,
    )
```

```python
import functools

import jax
import jax.numpy as jnp
from jax import lax
from jax.experimental import pallas as pl
from jax.experimental.pallas import tpu as pltpu
from jax.sharding import Mesh
from jax.sharding import PartitionSpec as P

HEADS = 64
KV_HEADS = 8
HEAD_DIM = 128
BLOCK = 128
LOG2E = 1.4426950408889634
CHUNK = 4
GROUP_HEADS = 2
PIECE = 512
WAVE = 8
FIRST_STEPS = 4


def pack_kernel(keys, values, out):
    for h in range(out.shape[0]):
        at = slice(h * HEAD_DIM, (h + 1) * HEAD_DIM)
        out[h, :, :HEAD_DIM] = keys[:, at]
        out[h, :, HEAD_DIM:] = values[:, at].T


def pack(keys, values, parts):
    tokens = keys.shape[0]
    vmem = pl.BlockSpec(memory_space=pltpu.VMEM)
    return pl.pallas_call(
        pack_kernel,
        in_specs=[vmem, vmem],
        out_specs=vmem,
        out_shape=jax.ShapeDtypeStruct((parts, tokens, 2 * HEAD_DIM), keys.dtype),
    )(keys, values)


def plan_kernel(place_ref, codes_ref, counts_ref, list_ref, fill_ref, *, blocks, sizes, zero, far):
    x_size, y_lo_size, core_size = sizes[:3]
    x, y, core = place_ref[0], place_ref[1], place_ref[2]
    shard = (x * y_lo_size + y) * core_size + core
    for a in range(blocks):
        list_ref[a, 0] = a
        list_ref[blocks + a, 0] = a
        fill_ref[a] = 1

    y_hi, z = place_ref[3], place_ref[4]
    y_size, z_size = sizes[3:]
    for step, (dy, dz) in enumerate(far):
        for row, sign in ((1, 1), (2, -1)):
            to_y = lax.rem(y_hi + sign * dy + y_size, y_size)
            to_z = lax.rem(z + sign * dz + z_size, z_size)
            list_ref[2 * blocks + row, step] = to_y * z_size + to_z

    def visit_shard(slot, _):
        from_x = lax.rem(x + lax.rem(slot, x_size), x_size)
        from_y = lax.rem(y + lax.rem(lax.div(slot, x_size), y_lo_size), y_lo_size)
        from_core = lax.rem(core + lax.div(slot, x_size * y_lo_size), core_size)
        j = (from_x * y_lo_size + from_y) * core_size + from_core

        def visit_entry(c, _):
            code = codes_ref[shard, j, c]
            a = lax.div(code, blocks)
            block = slot * blocks + lax.rem(code, blocks)
            at = fill_ref[a]
            list_ref[a, at] = block
            list_ref[blocks + a, at] = block
            fill_ref[a] = at + 1
            return 0

        return lax.fori_loop(0, counts_ref[shard, j], visit_entry, 0)

    lax.fori_loop(0, x_size * y_lo_size * core_size, visit_shard, 0)
    for a in range(blocks):
        filled = fill_ref[a]
        chunks = lax.div(filled + CHUNK - 1, CHUNK)
        list_ref[2 * blocks, a] = chunks

        def pad(at, _):
            list_ref[a, at] = a
            list_ref[blocks + a, at] = zero
            return 0

        lax.fori_loop(filled, chunks * CHUNK, pad, 0)


def plan(place, live_keys, live_count, blocks, sizes, zero, far):
    shards = live_keys.shape[0]
    width = -(-(shards * blocks + 1) // CHUNK) * CHUNK
    smem = pl.BlockSpec(memory_space=pltpu.SMEM)
    return pl.pallas_call(
        functools.partial(plan_kernel, blocks=blocks, sizes=sizes, zero=zero, far=far),
        in_specs=[smem] * 3,
        out_specs=smem,
        out_shape=jax.ShapeDtypeStruct((2 * blocks + 3, width), jnp.int32),
        scratch_shapes=[pltpu.SMEM((blocks,), jnp.int32)],
        cost_estimate=pl.CostEstimate(flops=0, bytes_accessed=20_000_000, transcendentals=0),
    )(place, live_keys, live_count)


def attend_kernel(listed, queries, *refs, blocks, steps, heads, shards, loads):
    if loads:
        pieces, (out, pairs, *rest) = refs[:shards], refs[shards:]
    else:
        pairs, out, *rest = refs
    ones, total, peak, *rest = rest
    groups = heads // GROUP_HEADS
    raw, soft, (level, fade, late_fade, *loading) = rest[:groups], rest[groups : groups + 2], rest[groups + 2 :]
    count = pairs.shape[0] - 1
    span = count // shards
    width = GROUP_HEADS * BLOCK
    scale = HEAD_DIM**-0.5 * LOG2E
    cuts = [slice(j * PIECE, (j + 1) * PIECE) for j in range(CHUNK * BLOCK // PIECE)]
    square = (BLOCK, BLOCK)
    unit = (
        lax.broadcasted_iota(jnp.int32, square, 0) == lax.broadcasted_iota(jnp.int32, square, 1)
    ).astype(jnp.bfloat16)

    def block_of(step):
        return listed[2 * blocks + 1, step]

    def arrival(j):
        return pltpu.make_async_copy(pieces[j], pairs.at[pl.ds(j * span, span)], loading[1].at[j])

    def arrive(b, i):
        ready = loading[0]
        last = lax.div(listed[b, i * CHUNK + CHUNK - 1], span) + 1
        needed = jnp.where(i >= listed[2 * blocks, b] - 1, shards, last)
        for j in range(shards):

            @pl.when((j >= ready[0]) & (j < needed))
            def _():
                arrival(j).wait()
                if j + WAVE < shards:
                    arrival(j + WAVE).start()

        ready[0] = jnp.maximum(ready[0], needed)

    def rows_of(b):
        return pl.ds(pl.multiple_of(b * BLOCK, BLOCK), BLOCK)

    def columns(g):
        return slice(g * width, (g + 1) * width)

    def keys_of(b, i):
        return jnp.concatenate([pairs[listed[b, i * CHUNK + c], :, :HEAD_DIM] for c in range(CHUNK)], axis=0)

    def values_of(b, i):
        slots = [listed[blocks + b, i * CHUNK + c] for c in range(CHUNK)]
        return jnp.concatenate(
            [
                jnp.concatenate([pairs[s, :, HEAD_DIM:] for s in slots], axis=1),
                jnp.concatenate([ones[(s == count).astype(jnp.int32)] for s in slots], axis=1),
            ],
            axis=0,
        )

    def score(b, keys, g):
        first = g * GROUP_HEADS
        tile = jnp.concatenate(
            [
                queries[rows_of(b), h * HEAD_DIM : (h + 1) * HEAD_DIM]
                for h in range(first, first + GROUP_HEADS)
            ],
            axis=0,
        )
        return lax.dot_general(keys, tile, (((1,), (1,)), ((), ())), preferred_element_type=jnp.float32)

    def partial_max(piece):
        return jnp.max(piece.reshape(-1, 8, width), axis=0)

    def first_scores(b):
        keys = keys_of(b, 0)
        for g in range(2):
            raw[g][...] = score(b, keys, g)

    def reset():
        total[...] = jnp.zeros(total.shape, jnp.float32)
        peak[...] = jnp.full(peak.shape, -jnp.inf, jnp.float32)
        soft[1][...] = jnp.zeros(soft[1].shape, jnp.bfloat16)
        late_fade[...] = jnp.ones(late_fade.shape, jnp.float32)
        level[...] = jnp.max(partial_max(raw[0][...]), axis=0, keepdims=True) * scale
        peak[:, columns(0)] = level[...]
        fade[...] = jnp.zeros(fade.shape, jnp.float32)

    ones[0] = jnp.ones(ones.shape[1:], jnp.bfloat16)
    ones[1] = jnp.zeros(ones.shape[1:], jnp.bfloat16)
    if loads:
        for j in range(WAVE):
            arrival(j).start()
        loading[0][0] = 0
        pairs[count] = jnp.zeros(pairs.shape[1:], jnp.bfloat16)
        arrive(block_of(steps[0]), 0)
    first_scores(block_of(steps[0]))
    reset()

    def visit_block(step, _):
        b = block_of(step)
        end = listed[2 * blocks, b]

        def visit(i, _):
            following = jnp.minimum(i + 1, end - 1)

            if loads:

                @pl.when(step == steps[0])
                def _():
                    arrive(b, following)

            keys = keys_of(b, i)
            next_keys = keys_of(b, following)
            values = values_of(b, i)
            before = values_of(b, jnp.maximum(i - 1, 0))
            new, factor, late = level[...], fade[...], late_fade[...]
            for g in range(groups):
                ahead, upcoming, done = (g + 2) % groups, (g + 1) % groups, (g - 1) % groups
                source = keys if g + 2 < groups else next_keys
                multiplier = values if g else before
                into = columns(done)
                total[:, into] = total[:, into] * late
                tops = None
                for cut in cuts:
                    raw[ahead][cut, :] = score(b, source[cut, :], ahead)
                    soft[g % 2][cut, :] = jnp.exp2(raw[g][cut, :] * scale - new).astype(jnp.bfloat16)
                    total[:, into] += jnp.dot(
                        multiplier[:, cut], soft[(g + 1) % 2][cut, :], preferred_element_type=jnp.float32
                    )
                    most = partial_max(raw[upcoming][cut, :])
                    tops = most if tops is None else jnp.maximum(tops, most)
                at = columns(upcoming)
                old = peak[:, at]
                new = jnp.maximum(old, jnp.max(tops, axis=0, keepdims=True) * scale)
                peak[:, at] = new
                factor, late = jnp.exp2(old - new), factor
            level[...] = new
            fade[...] = factor
            late_fade[...] = late
            return 0

        lax.fori_loop(0, end, visit, 0)
        at = columns(groups - 1)
        total[:, at] = total[:, at] * late_fade[...] + jnp.dot(
            values_of(b, end - 1), soft[1][...], preferred_element_type=jnp.float32
        )
        first_scores(block_of(jnp.minimum(step + 1, steps[1] - 1)))
        for h in range(heads):
            at = slice(h * BLOCK, (h + 1) * BLOCK)
            inverse = 1.0 / total[HEAD_DIM : HEAD_DIM + 1, at]
            normed = (total[:HEAD_DIM, at] * inverse).astype(jnp.bfloat16)
            turned = lax.dot_general(
                unit, normed, (((1,), (1,)), ((), ())), preferred_element_type=jnp.float32
            )
            out[rows_of(step - steps[0]), h * HEAD_DIM : (h + 1) * HEAD_DIM] = turned.astype(jnp.bfloat16)
        reset()
        return 0

    lax.fori_loop(*steps, visit_block, 0)


def attend(queries, sources, lists, steps):
    rows, width = queries.shape
    heads = width // HEAD_DIM
    blocks = rows // BLOCK
    loads = isinstance(sources, list)
    pair_estimate = 22 * (steps[1] - steps[0]) * 2 * 2 * heads * BLOCK * BLOCK * HEAD_DIM
    vmem = pl.BlockSpec(memory_space=pltpu.VMEM)
    out_specs, out_shape = [vmem], [jax.ShapeDtypeStruct(((steps[1] - steps[0]) * BLOCK, width), jnp.bfloat16)]
    if loads:
        shards = len(sources)
        span = sources[0].shape[0] // BLOCK
        count = shards * span
        sources = [
            pltpu.with_memory_space_constraint(piece.reshape(span, BLOCK, -1), pltpu.HBM) for piece in sources
        ]
        in_specs = [pl.BlockSpec(memory_space=pl.ANY)] * shards
        loading = [pltpu.SMEM((1,), jnp.int32), pltpu.SemaphoreType.DMA((shards,))]
        out_specs.append(vmem)
        out_shape.append(jax.ShapeDtypeStruct((count + 1, BLOCK, 2 * HEAD_DIM), jnp.bfloat16))
    else:
        shards = (sources.shape[0] - 1) // blocks
        sources, in_specs, loading = [sources], [vmem], []
    return pl.pallas_call(
        functools.partial(
            attend_kernel, blocks=blocks, steps=steps, heads=heads, shards=shards, loads=loads
        ),
        in_specs=[pl.BlockSpec(memory_space=pltpu.SMEM), vmem, *in_specs],
        out_specs=out_specs,
        scratch_shapes=[
            pltpu.VMEM((2, 16, BLOCK), jnp.bfloat16),
            pltpu.VMEM((HEAD_DIM + 16, heads * BLOCK), jnp.float32),
            pltpu.VMEM((1, heads * BLOCK), jnp.float32),
        ]
        + [pltpu.VMEM((CHUNK * BLOCK, GROUP_HEADS * BLOCK), jnp.float32)] * (heads // GROUP_HEADS)
        + [pltpu.VMEM((CHUNK * BLOCK, GROUP_HEADS * BLOCK), jnp.bfloat16)] * 2
        + [pltpu.VMEM((1, GROUP_HEADS * BLOCK), jnp.float32)] * 3
        + loading,
        out_shape=out_shape,
        compiler_params=pltpu.CompilerParams(vmem_limit_bytes=32 * 1024 * 1024),
        cost_estimate=pl.CostEstimate(flops=pair_estimate * 3, bytes_accessed=6_000_000, transcendentals=0),
    )(lists, pltpu.with_memory_space_constraint(queries, pltpu.VMEM), *sources)


def assemble_kernel(listed, *refs):
    *parts, late, out, sem = refs
    tokens, width = out.shape[0], late.shape[1]
    count = out.shape[1] // width
    copies = []
    for r in range(count):
        at = pl.ds(pl.multiple_of(listed[2 * count + 2, r] * width, width), width)
        source = parts[r] if r < len(parts) else late.at[pl.ds(late.shape[0] - tokens, tokens)]
        copies.append(pltpu.make_async_copy(source, out.at[:, at], sem.at[r]))
    for copy in copies:
        copy.start()
    for copy in copies:
        copy.wait()


def assemble(lists, parts, late):
    rows, width = parts[0].shape
    count = len(parts) + 1
    parts = [*parts[:FIRST_STEPS]] + [
        pltpu.with_memory_space_constraint(part, pltpu.VMEM) for part in [*parts[FIRST_STEPS:], late]
    ]
    return pl.pallas_call(
        assemble_kernel,
        in_specs=[pl.BlockSpec(memory_space=pltpu.SMEM)]
        + [pl.BlockSpec(memory_space=pltpu.VMEM)] * FIRST_STEPS
        + [pl.BlockSpec(memory_space=pl.ANY)] * (count - FIRST_STEPS),
        out_specs=pl.BlockSpec(memory_space=pl.ANY),
        out_shape=jax.ShapeDtypeStruct((rows, width * count), late.dtype),
        scratch_shapes=[pltpu.SemaphoreType.DMA((count,))],
    )(lists, *parts)


def shift(array, axis, step):
    size = lax.axis_size(axis)
    return lax.ppermute(array, axis, [(i, (i + step) % size) for i in range(size)])


def gather_shards(own):
    across = shift(own, "y_lo", 1)
    up, down = shift(own, "x", -1), shift(own, "x", 1)
    here = [own, up, shift(down, "x", 1), down]
    there = [across, shift(across, "x", -1), None, shift(across, "x", 1)]
    up_too, down_too = shift(up, "core", 1), shift(down, "core", 1)
    there[1], up_too, down_too = lax.optimization_barrier((there[1], up_too, down_too))
    there[2] = shift(there[1], "x", -1)
    other = [shift(own, "core", 1), up_too, shift(here[2], "core", 1), down_too]
    return here + there + other + [shift(piece, "core", 1) for piece in there]


def local(queries, keys, values, live_keys, live_count):
    head_axes, blk_axes = ("y_hi", "z"), ("x", "y_lo", "core")
    parts = lax.axis_size(head_axes)
    tokens = queries.shape[0]
    sizes = tuple(lax.axis_size(axis) for axis in blk_axes + head_axes)
    blocks = parts * tokens // BLOCK

    def exchange(cut):
        moved = lax.all_to_all(cut, head_axes, split_axis=0, concat_axis=0, tiled=True)
        return moved.reshape(parts * tokens, -1)

    def cut(array):
        return array.reshape(tokens, parts, -1)

    own = exchange(pack(keys, values, parts))
    y_size, z_size = (lax.axis_size(axis) for axis in head_axes)
    far = [(dy, dz) for dy in range(y_size) for dz in range(z_size)]
    far.sort(key=lambda d: (2 * d[0] + min(d[1], z_size - d[1]), d[0]), reverse=True)

    def at_distance(y, z, dy, dz):
        return (y + dy) % y_size * z_size + (z + dz) % z_size

    place = jnp.stack([lax.axis_index(axis) for axis in blk_axes + head_axes]).astype(jnp.int32)
    lists = plan(place, live_keys, live_count, blocks, sizes, live_keys.shape[0] * blocks, far)
    own, lists, query_parts = lax.optimization_barrier((own, lists, cut(queries).transpose(1, 0, 2)))
    pieces = gather_shards(own)
    query_local = exchange(query_parts)

    def send(attended, steps):
        sent = []
        for step in range(*steps):
            part = attended[(step - steps[0]) * tokens : (step - steps[0] + 1) * tokens]
            pairs = [(k, at_distance(k // z_size, k % z_size, *far[step])) for k in range(y_size * z_size)]
            sent.append(lax.ppermute(part, head_axes, pairs))
        return sent

    early, late = (0, FIRST_STEPS), (FIRST_STEPS, parts)
    attended, gathered = attend(query_local, pieces, lists, early)
    received = send(attended, early)
    (attended,) = attend(query_local, gathered, lists, late)
    attended, received = lax.optimization_barrier((attended, received))
    received += send(attended, (FIRST_STEPS, parts - 1))
    return assemble(lists, received, attended)


def solution(mesh):
    fine = Mesh(mesh.devices.reshape(4, 2, 2, 2, 4), ("x", "y_lo", "core", "y_hi", "z"))
    rows = P(("x", "y_lo", "core", "y_hi", "z"), None)
    return jax.shard_map(
        local,
        mesh=fine,
        in_specs=(rows, rows, rows, P(), P()),
        out_specs=rows,
        check_vma=False,
    )
```
